128 devices in a mesh: rep: 16 (over x, z), tp: 8 (over y, core).
Axes of the slice: x: 4, y: 4, z: 4, core: 2. Of those that a mesh axis runs over, the one named last changes fastest.
Arguments:
- inputs: bfloat16 [16384, 1024], P(('rep', 'tp')), may hold values from -6 to 6
- cotangent: bfloat16 [16384, 1024], P(('rep', 'tp')), may hold values from -0.29882812 to 0.29882812
- weight_in: bfloat16 [2, 1024, 4, 8, 128], P(None, None, None, 'tp'), may hold values from -0.1875 to 0.1875
- weight_out: bfloat16 [2, 8, 128, 1024], P(None, 'tp'), may hold values from -0.1875 to 0.1875
- bias_table: float32 [2, 8, 16], P(None, 'tp'), may hold values from -4 to 4
- lengths: int32 [16], P('rep'), may hold values from 256 to 1024, as said below
- stamps: int32 [16, 1024], P('rep'), may hold values from 0 to 111, as said below
- factor_in: float32 [2, 8, 32, 512], P(None, 'tp'), may hold values from -6 to 6
- factor_out: float32 [2, 8, 32, 1024], P(None, 'tp'), may hold values from -6 to 6
- error_in: float32 [16, 2, 8, 1024, 512], P('rep', None, 'tp'), may hold values from -3 to 3
- error_out: float32 [16, 2, 8, 128, 1024], P('rep', None, 'tp'), may hold values from -3 to 3
Outputs:
- update_in: float32 [2, 8, 1024, 512], P(None, 'tp')
- update_out: float32 [2, 8, 128, 1024], P(None, 'tp')
- factor_in_next: float32 [2, 8, 32, 512], P(None, 'tp')
- factor_out_next: float32 [2, 8, 32, 1024], P(None, 'tp')
- error_in_next: float32 [16, 2, 8, 1024, 512], P('rep', None, 'tp')
- error_out_next: float32 [16, 2, 8, 128, 1024], P('rep', None, 'tp')
The draws below stay inside these ranges and needn't reach their ends.
Inputs may be any that keep to these rules, and one draw needn't show every extreme that they name: `lengths`: A sequence's events are its first length positions; some sequence has exactly 1024. `stamps`: non-decreasing along each sequence; within a sequence the stamps rise by at most 48 from the first to the last event.
All inputs are finite; a program needn't handle non-finite values.
Results may differ from the reference program's by a relative error of at most 0.04.
Values may be sent and summed in bfloat16 or wider, within the bound.
No kernel may reach another device: no remote copies, remote signals or barrier semaphores. Data moves between devices by JAX's collectives and lax.ppermute only.
A program may use at most 128 MiB of HBM per device.

```python
import jax
import jax.numpy as jnp
from jax import lax

D = 1024
HEADS = 8
HD = 128
R = 32
NB = 16
LEN = 1024
LAYERS = 2
SEQS_DEV = 1
REPS = 16
SEQUENCES = 16
TOKENS = 16384
N_REP = 16
N_TP = 8


def draw_lengths(key, part):
    key = jax.random.fold_in(key, 11)
    first, second = jax.random.split(key)
    values = jax.random.randint(first, (SEQUENCES,), LEN // 4, LEN + 1)
    chosen = jax.random.randint(second, (), 0, SEQUENCES)
    return jnp.where(lax.iota(jnp.int32, SEQUENCES) == chosen, LEN, values).astype(jnp.int32)


def draw_stamps(key, part):
    key = jax.random.fold_in(key, 23)
    first, second, third = jax.random.split(key, 3)
    ceiling = min(3 * NB, LEN // 2)
    rows = lax.iota(jnp.int32, SEQUENCES)
    places = lax.iota(jnp.int32, LEN)
    chosen = jax.random.randint(third, (), 0, SEQUENCES)
    partner = (chosen + 1) % SEQUENCES
    anchor = jax.random.randint(first, (SEQUENCES,), 0, 64)
    anchor = jnp.where(rows == chosen, 63, jnp.where(rows == partner, 0, anchor))
    rises = jnp.where(jax.random.randint(second, (SEQUENCES, LEN), 0, LEN) < ceiling, 1, 0)
    forced = (rows[:, None] == chosen) & (places[None, :] >= LEN - ceiling)
    rises = jnp.where(forced, 1, rises)
    climbed = jnp.minimum(jnp.cumsum(rises, axis=1), ceiling)
    return (anchor[:, None] + climbed).astype(jnp.int32)


def level_of(key, dims, shards, least, largest):
    def one(position, blocks):
        heights = jax.random.uniform(jax.random.fold_in(jax.random.fold_in(key, 6), position), (blocks,), jnp.float32, least / len(shards), largest / len(shards))
        return jnp.repeat(jnp.exp(heights), dims[position] // blocks).reshape((-1,) + (1,) * (len(dims) - position - 1))

    gain = one(*shards[0])
    for cut in shards[1:]:
        gain = gain * one(*cut)
    return gain


def scatter_about(own_key, extent, deviation, reach, cuts=(), dtype=jnp.bfloat16):
    gain = level_of(own_key, extent, cuts, -0.22, 0.18) if cuts else 1.0
    entries = jax.random.normal(own_key, extent, jnp.float32) * deviation * gain
    return jnp.minimum(jnp.maximum(entries, -reach), reach).astype(dtype)


def setup_inputs(seed: int = 0) -> dict:
    seeds = jax.random.split(jax.random.key(seed), 12)
    inputs = scatter_about(seeds[0], (TOKENS, D), 1.0, 6.0, ((0, 128),))
    cotangent = scatter_about(seeds[1], (TOKENS, D), 0.05, 0.29882812, ((0, 128),))
    weight_in = scatter_about(seeds[2], (LAYERS, D, 4, HEADS, HD), D ** -0.5, 0.1875, ((3, 8),))
    weight_out = scatter_about(seeds[3], (LAYERS, HEADS, HD, D), (HEADS * HD) ** -0.5, 0.1875, ((1, 8),))
    bias_table = scatter_about(seeds[4], (LAYERS, HEADS, NB), 1.0, 4.0, ((1, 8),), jnp.float32)
    lengths = draw_lengths(jax.random.fold_in(seeds[11], 71), 0)
    stamps = draw_stamps(jax.random.fold_in(seeds[11], 71), 0)
    factor_in = scatter_about(seeds[7], (LAYERS, HEADS, R, 4 * HD), 1.0, 6.0, ((1, 8),), jnp.float32)
    factor_out = scatter_about(seeds[8], (LAYERS, HEADS, R, D), 1.0, 6.0, ((1, 8),), jnp.float32)
    error_in = scatter_about(seeds[9], (REPS, LAYERS, HEADS, D, 4 * HD), 0.5, 3.0, ((0, 16), (2, 8)), jnp.float32)
    error_out = scatter_about(seeds[10], (REPS, LAYERS, HEADS, HD, D), 0.5, 3.0, ((0, 16), (2, 8)), jnp.float32)
    return {"inputs": inputs, "cotangent": cotangent, "weight_in": weight_in, "weight_out": weight_out, "bias_table": bias_table, "lengths": lengths, "stamps": stamps, "factor_in": factor_in, "factor_out": factor_out, "error_in": error_in, "error_out": error_out}


epsilon = 1e-05
highest = lax.Precision.HIGHEST

def to_half(values):
    return lax.optimization_barrier(values.astype(jnp.bfloat16))

def silu_slope(argument):
    sigmoid_v = jax.nn.sigmoid(argument)
    return sigmoid_v * (1.0 + argument * (1.0 - sigmoid_v))

def normalize(features):
    average = lax.optimization_barrier(jnp.mean(features, axis=-1, keepdims=True))
    centred = features - average
    inverse = lax.rsqrt(lax.optimization_barrier(jnp.mean(centred * centred, axis=-1, keepdims=True)) + epsilon)
    return (centred * inverse, inverse)

def normalize_back(features, upstream):
    normed, inverse = normalize(features)
    return inverse * (upstream - lax.optimization_barrier(jnp.mean(upstream, axis=-1, keepdims=True)) - normed * lax.optimization_barrier(jnp.mean(upstream * normed, axis=-1, keepdims=True)))

def time_bias(lookup, stamps):
    highest_bucket = lookup.shape[-1] - 1
    distance = jnp.clip(stamps[:, None] - stamps[None, :], 0, highest_bucket)
    gathered_bias = jnp.zeros((lookup.shape[0],) + distance.shape, jnp.float32)
    for bucket in range(highest_bucket + 1):
        gathered_bias = jnp.where((distance == bucket)[None], lookup[:, bucket][:, None, None], gathered_bias)
    return gathered_bias

def attend(activity, lookup, stamps, length):
    parts = activity.astype(jnp.float32)
    gate_part, value_part, query_part, key_part = (parts[:, 0], parts[:, 1], parts[:, 2], parts[:, 3])
    scaling = query_part.shape[-1] ** (-0.5)
    scores = jnp.einsum('ihk,jhk->hij', query_part, key_part) * scaling + time_bias(lookup, stamps)
    places = lax.iota(jnp.int32, activity.shape[0])
    allowed = ((places[None, :] <= places[:, None]) & (places[:, None] < length))[None]
    seq_count = length.astype(jnp.float32)
    weights = to_half(jnp.where(allowed, jax.nn.silu(scores), 0.0) / seq_count).astype(jnp.float32)
    attended = jnp.einsum('hij,jhk->ihk', weights, value_part)
    normed, inverse = normalize(attended)
    return (gate_part, value_part, query_part, key_part, scaling, scores, allowed, seq_count, weights, normed, inverse)

def mix_forward(activity, lookup, stamps, length):
    parts = attend(activity, lookup, stamps, length)
    return to_half(parts[9] * parts[0])

def mix_backward(activity, lookup, stamps, length, upstream):
    gate_part, value_part, query_part, key_part, scaling, scores, allowed, seq_count, weights, normed, inverse = attend(activity, lookup, stamps, length)
    grad_gate = upstream * normed
    grad_normed = upstream * gate_part
    grad_attended = inverse * (grad_normed - lax.optimization_barrier(jnp.mean(grad_normed, axis=-1, keepdims=True)) - normed * lax.optimization_barrier(jnp.mean(grad_normed * normed, axis=-1, keepdims=True)))
    grad_attended = to_half(grad_attended).astype(jnp.float32)
    grad_weights = jnp.einsum('ihk,jhk->hij', grad_attended, value_part)
    grad_value = jnp.einsum('hij,ihk->jhk', weights, grad_attended)
    grad_scores = to_half(jnp.where(allowed, grad_weights * silu_slope(scores), 0.0) / seq_count).astype(jnp.float32)
    grad_query = jnp.einsum('hij,jhk->ihk', grad_scores, key_part) * scaling
    grad_key = jnp.einsum('hij,ihk->jhk', grad_scores, query_part) * scaling
    return jnp.stack([grad_gate, grad_value, grad_query, grad_key], axis=1)

def group_sum(partials):
    return lax.optimization_barrier(jnp.sum(to_half(partials).astype(jnp.float32), axis=0))

def replica_grads(inputs, cotangent, weight_in, weight_out, bias_table, lengths, stamps):
    row_count = inputs.shape[0]
    per_group = HEADS // N_TP
    stream = inputs.astype(jnp.float32)
    stored = []
    for layer_index in range(LAYERS):
        normed = to_half(normalize(stream)[0])
        projected = jnp.dot(normed.astype(jnp.float32), weight_in[layer_index].reshape(D, -1).astype(jnp.float32), preferred_element_type=jnp.float32).reshape(row_count, 4, HEADS, HD)
        activity = to_half(jax.nn.silu(projected))
        lookup = bias_table[layer_index]
        gated_rows = lax.map(lambda member: mix_forward(member[0], lookup, member[1], member[2]), (activity.reshape(SEQS_DEV, LEN, 4, HEADS, HD), stamps, lengths))
        gated_rows = gated_rows.reshape(row_count, HEADS, HD)
        partials = jnp.einsum('rgc,gcd->grd', gated_rows.reshape(row_count, N_TP, -1).astype(jnp.float32), weight_out[layer_index].reshape(N_TP, -1, D).astype(jnp.float32))
        stored.append((stream, normed, projected, activity, gated_rows))
        stream = stream + group_sum(partials)
    grad_stream = cotangent.astype(jnp.float32)
    grads_in = []
    grads_out = []
    for layer_index in reversed(range(LAYERS)):
        stream_here, normed, projected, activity, gated_rows = stored[layer_index]
        lookup = bias_table[layer_index]
        grad_mixture = to_half(grad_stream).astype(jnp.float32)
        grads_out.insert(0, jnp.einsum('rhk,rd->hkd', gated_rows.astype(jnp.float32), grad_mixture).astype(jnp.bfloat16))
        grad_gated = jnp.dot(grad_mixture, weight_out[layer_index].reshape(-1, D).astype(jnp.float32).T).reshape(SEQS_DEV, LEN, HEADS, HD)
        grad_activity = lax.map(lambda member: mix_backward(member[0], lookup, member[1], member[2], member[3]), (activity.reshape(SEQS_DEV, LEN, 4, HEADS, HD), stamps, lengths, grad_gated))
        grad_projected = to_half(grad_activity.reshape(row_count, 4, HEADS, HD) * silu_slope(projected)).astype(jnp.float32)
        grads_in.insert(0, jnp.einsum('rd,rchk->hdck', normed.astype(jnp.float32), grad_projected).astype(jnp.bfloat16).reshape(HEADS, D, 4 * HD))
        if layer_index > 0:
            partials = jnp.einsum('rcgek,dcgek->grd', grad_projected.reshape(row_count, 4, N_TP, per_group, HD), weight_in[layer_index].reshape(D, 4, N_TP, per_group, HD).astype(jnp.float32))
            grad_stream = grad_stream + normalize_back(stream_here, group_sum(partials))
    return (jnp.stack(grads_in), jnp.stack(grads_out))

def orthonormal(factors):
    gram = jnp.einsum('lhrn,lhsn->lhrs', factors, factors, precision=highest)
    lower = jnp.linalg.cholesky(gram)
    return lax.linalg.triangular_solve(lower, factors, left_side=True, lower=True)

def compress(grads, errors, starting):
    merged = grads.astype(jnp.float32) + errors
    left = jnp.einsum('lhrm,alhnm->lhrn', starting, merged, precision=highest)
    basis = orthonormal(left)
    right = jnp.einsum('lhrn,alhnm->lhrm', basis, merged, precision=highest) / N_REP
    update = jnp.einsum('lhrn,lhrm->lhnm', basis, right, precision=highest)
    return (update, right, merged - update[None])

def reference(inputs, cotangent, weight_in, weight_out, bias_table, lengths, stamps, factor_in, factor_out, error_in, error_out):
    row_count = SEQS_DEV * LEN
    shaped = (inputs.reshape(N_REP, row_count, D), cotangent.reshape(N_REP, row_count, D), lengths.reshape(N_REP, SEQS_DEV), stamps.reshape(N_REP, SEQS_DEV, LEN))
    grads_in, grads_out = lax.map(lambda member: replica_grads(member[0], member[1], weight_in, weight_out, bias_table, member[2], member[3]), shaped)
    update_in, next_in, error_in_next = compress(grads_in, error_in, factor_in)
    update_out, next_out, error_out_next = compress(grads_out, error_out, factor_out)
    return (update_in, update_out, next_in, next_out, error_in_next, error_out_next)
```

```python
import functools

import jax
import jax.numpy as jnp
from jax import lax
from jax.experimental import pallas as pl
from jax.experimental.pallas import tpu as pltpu
from jax.sharding import PartitionSpec as P

epsilon = 1e-05
highest = lax.Precision.HIGHEST
half = jnp.bfloat16
full = jnp.float32

TOKENS = 1024
WIDTH = 1024
HEAD = 128
WIDE = 4 * HEAD
RANK = 32
BUCKETS = 16
OWN = 128
BLOCK = 256
BLOCKS = TOKENS // BLOCK
VMEM_BYTES = 56 * 1024 * 1024

whole = pl.BlockSpec(memory_space=pltpu.VMEM)
scalars = pl.BlockSpec(memory_space=pltpu.SMEM)


def nn(a, b):
    return jnp.dot(a, b, preferred_element_type=full)


def nt(a, b, precision=None):
    return lax.dot_general(
        a, b, (((1,), (1,)), ((), ())), preferred_element_type=full, precision=precision
    )


def tn(a, b, precision=None):
    return lax.dot_general(
        a, b, (((0,), (0,)), ((), ())), preferred_element_type=full, precision=precision
    )


def logistic(x):
    return 0.5 * jnp.tanh(0.5 * x) + 0.5


def silu_slope(x):
    s = logistic(x)
    return s * (1.0 + x * (1.0 - s))


def centre(x):
    c = x - jnp.mean(x, axis=-1, keepdims=True)
    inverse = lax.rsqrt(jnp.mean(c * c, axis=-1, keepdims=True) + epsilon)
    return c * inverse, inverse


def split(x):
    high = x.astype(half)
    return high, (x - high.astype(full)).astype(half)


def call(body, name, flops, moved, operands, in_specs, outs, scratch, out_specs=None):
    grid = {} if all(spec.block_shape is None for spec in in_specs) else {"grid": (1,)}
    return pl.pallas_call(
        body,
        name=name,
        **grid,
        out_shape=outs,
        in_specs=in_specs,
        out_specs=out_specs if out_specs is not None else [whole] * len(outs),
        scratch_shapes=scratch,
        compiler_params=pltpu.CompilerParams(vmem_limit_bytes=VMEM_BYTES),
        cost_estimate=pl.CostEstimate(flops=flops, bytes_accessed=moved, transcendentals=0),
    )(*operands)


def shape(dims, dtype):
    return jax.ShapeDtypeStruct(dims, dtype)


def placed(device, position):
    base = device if position < 4 else device + 1 - 2 * lax.rem(device, 2)
    return lax.rem(base + 2 * (position % 4), 8)


def rows_of(device, position):
    return pl.ds(pl.multiple_of(placed(device, position) * OWN, OWN), OWN)


def attention_operands(stamps_ref, table_ref, query_of, key_of, qa_ref, ka_ref):
    scale = HEAD**-0.5
    places = lax.broadcasted_iota(jnp.int32, (HEAD, HEAD), 0)
    lanes = lax.broadcasted_iota(jnp.int32, (HEAD, HEAD), 1)
    gap = jnp.clip(places - (lanes & 63), 0, BUCKETS - 1)
    lookup = jnp.zeros((HEAD, HEAD), full)
    for bucket in range(BUCKETS):
        lookup = jnp.where(gap == bucket, table_ref[0, bucket] * (1.0 / scale), lookup)
    high = lookup.astype(half).astype(full)
    lookup = jnp.where(lanes < 64, high, lookup - high)
    lookup = jnp.where(places < 64, lookup, 0.0).astype(half)
    first = stamps_ref[0:1, :]
    for part in range(BLOCKS):
        rows = slice(part * BLOCK, (part + 1) * BLOCK)
        since = stamps_ref[rows, :] - first
        columns = lax.broadcasted_iota(jnp.int32, (BLOCK, HEAD), 1)
        hot = jnp.where(since == (columns & 63), 1.0, 0.0)
        left_hot = jnp.where(columns < 64, hot, 0.0).astype(half)
        qa_ref[rows, HEAD:] = nn(left_hot, lookup).astype(half)
        ka_ref[rows, HEAD:] = hot.astype(half)
        qa_ref[rows, :HEAD] = query_of(rows)
        ka_ref[rows, :HEAD] = key_of(rows)


def score_block(qa_ref, ka_ref, i, j):
    return nt(
        qa_ref[i * BLOCK : (i + 1) * BLOCK, :], ka_ref[j * BLOCK : (j + 1) * BLOCK, :]
    ) * (HEAD**-0.5)


def causal():
    return lax.broadcasted_iota(jnp.int32, (BLOCK, BLOCK), 0) >= lax.broadcasted_iota(
        jnp.int32, (BLOCK, BLOCK), 1
    )


def row_mask(i, length):
    places = lax.broadcasted_iota(jnp.int32, (BLOCK, HEAD), 0) + i * BLOCK
    return places < length


def attend_forward(length, qa_ref, ka_ref, values_ref, proj_ref, gated_ref):
    share = 1.0 / length.astype(full)
    for i in range(BLOCKS):
        rows = slice(i * BLOCK, (i + 1) * BLOCK)
        total = jnp.zeros((BLOCK, HEAD), full)
        for j in range(i + 1):
            s = score_block(qa_ref, ka_ref, i, j)
            w = s * logistic(s)
            if i == j:
                w = jnp.where(causal(), w, 0.0)
            total += nn(w.astype(half), values_ref[j * BLOCK : (j + 1) * BLOCK, :])
        attended = jnp.where(row_mask(i, length), total * share, 0.0)
        normed, _ = centre(attended)
        gate = proj_ref[rows, :HEAD]
        gate = (gate * logistic(gate)).astype(half).astype(full)
        gated_ref[rows, :] = (normed * gate).astype(half)


def attend_backward(
    length,
    qa_ref,
    ka_ref,
    values_ref,
    proj_ref,
    upstream_of,
    gated_ref,
    grad_ref,
    weights_ref,
    slope_ref,
    dk_ref,
    dv_ref,
):
    share = 1.0 / length.astype(full)
    scale = HEAD**-0.5
    for i in range(BLOCKS):
        rows = slice(i * BLOCK, (i + 1) * BLOCK)
        total = jnp.zeros((BLOCK, HEAD), full)
        for j in range(i + 1):
            cols = slice(j * BLOCK, (j + 1) * BLOCK)
            s = score_block(qa_ref, ka_ref, i, j)
            sigmoid = logistic(s)
            w = s * sigmoid
            slope = sigmoid + w * (1.0 - sigmoid)
            if i == j:
                w = jnp.where(causal(), w, 0.0)
                slope = jnp.where(causal(), slope, 0.0)
            w = w.astype(half)
            weights_ref[:, cols] = w
            slope_ref[:, cols] = slope
            total += nn(w, values_ref[cols, :])
        inside = row_mask(i, length)
        attended = jnp.where(inside, total * share, 0.0)
        normed, inverse = centre(attended)
        gate_raw = proj_ref[rows, :HEAD]
        gate = (gate_raw * logistic(gate_raw)).astype(half).astype(full)
        gated_ref[rows, :] = (normed * gate).astype(half)
        upstream = upstream_of(rows)
        grad_ref[rows, :HEAD] = (upstream * normed * silu_slope(gate_raw)).astype(half)
        g = upstream * gate
        back = inverse * (
            g
            - jnp.mean(g, axis=-1, keepdims=True)
            - normed * jnp.mean(g * normed, axis=-1, keepdims=True)
        )
        back = jnp.where(inside, back, 0.0).astype(half)
        dq = jnp.zeros((BLOCK, HEAD), full)
        for j in range(i + 1):
            cols = slice(j * BLOCK, (j + 1) * BLOCK)
            ds = (nt(back, values_ref[cols, :]) * slope_ref[:, cols]).astype(half)
            dq += nn(ds, ka_ref[cols, :HEAD])
            dk = tn(ds, qa_ref[rows, :HEAD])
            dv = tn(weights_ref[:, cols], back)
            if i == j:
                dk_ref[cols, :] = dk
                dv_ref[cols, :] = dv
            else:
                dk_ref[cols, :] += dk
                dv_ref[cols, :] += dv
        raw = proj_ref[rows, 2 * HEAD : 3 * HEAD]
        grad_ref[rows, 2 * HEAD : 3 * HEAD] = (dq * (scale * share) * silu_slope(raw)).astype(half)
    for i in range(BLOCKS):
        rows = slice(i * BLOCK, (i + 1) * BLOCK)
        raw = proj_ref[rows, HEAD : 2 * HEAD]
        grad_ref[rows, HEAD : 2 * HEAD] = (dv_ref[rows, :] * share * silu_slope(raw)).astype(half)
        raw = proj_ref[rows, 3 * HEAD :]
        grad_ref[rows, 3 * HEAD :] = (dk_ref[rows, :] * (scale * share) * silu_slope(raw)).astype(
            half
        )


def silu_half(x):
    return (x * logistic(x)).astype(half)


def operands_from(proj_ref, stamps_ref, table_ref, qa_ref, ka_ref, values_ref):
    attention_operands(
        stamps_ref,
        table_ref,
        lambda rows: silu_half(proj_ref[rows, 2 * HEAD : 3 * HEAD]),
        lambda rows: silu_half(proj_ref[rows, 3 * HEAD :]),
        qa_ref,
        ka_ref,
    )
    for part in range(BLOCKS):
        rows = slice(part * BLOCK, (part + 1) * BLOCK)
        values_ref[rows, :] = silu_half(proj_ref[rows, HEAD : 2 * HEAD])


def first_forward(device_ref, length_ref, table_ref, stamps_ref, *refs):
    blocks = refs[:8]
    weight_ref, rows_ref, normed_ref, proj_ref, gated_ref, qa_ref, ka_ref, values_ref = refs[8:]
    device = device_ref[0]
    for position, block in enumerate(blocks):
        rows_ref[rows_of(device, position), :] = block[...]
    for part in range(BLOCKS):
        rows = slice(part * BLOCK, (part + 1) * BLOCK)
        normed = centre(rows_ref[rows, :].astype(full))[0].astype(half)
        normed_ref[rows, :] = normed
        proj_ref[rows, :] = nn(normed, weight_ref[...])
    operands_from(proj_ref, stamps_ref, table_ref, qa_ref, ka_ref, values_ref)
    attend_forward(length_ref[0], qa_ref, ka_ref, values_ref, proj_ref, gated_ref)


def second_layer(device_ref, length_ref, table_ref, stamps_ref, rows_ref, *refs):
    heads = refs[:8]
    mix_ref, weight_in_ref, cot_ref, weight_out_ref = refs[8:12]
    normed_ref, grad_ref, gated_ref, send_ref, keep_ref, stream_ref = refs[12:18]
    all_ref, proj_ref, qa_ref, ka_ref, values_ref = refs[18:23]
    weights_ref, slope_ref, dk_ref, dv_ref, whole_stream_ref = refs[23:]
    device = device_ref[0]
    for position, block in enumerate(heads):
        all_ref[:, rows_of(device, position)] = block[...]
    for part in range(BLOCKS):
        rows = slice(part * BLOCK, (part + 1) * BLOCK)
        stream = rows_ref[rows, :].astype(full) + nn(all_ref[rows, :], mix_ref[...])
        whole_stream_ref[rows, :] = stream
        normed = centre(stream)[0].astype(half)
        normed_ref[rows, :] = normed
        proj_ref[rows, :] = nn(normed, weight_in_ref[...])
    stream_ref[...] = whole_stream_ref[rows_of(device, 0), :]
    operands_from(proj_ref, stamps_ref, table_ref, qa_ref, ka_ref, values_ref)
    attend_backward(
        length_ref[0],
        qa_ref,
        ka_ref,
        values_ref,
        proj_ref,
        lambda rows: nt(cot_ref[rows, :], weight_out_ref[...]),
        gated_ref,
        grad_ref,
        weights_ref,
        slope_ref,
        dk_ref,
        dv_ref,
    )
    for position in range(4):
        out = slice(position * OWN, (position + 1) * OWN)
        keep_ref[out, :] = nt(grad_ref[rows_of(device, position), :], weight_in_ref[...]).astype(half)
        send_ref[out, :] = nt(
            grad_ref[rows_of(device, position + 4), :], weight_in_ref[...]
        ).astype(half)


def pair_sum(keep_ref, come_ref, a_ref, b_ref, c_ref, d_ref):
    for position, out in enumerate((a_ref, b_ref, c_ref, d_ref)):
        rows = slice(position * OWN, (position + 1) * OWN)
        out[...] = (keep_ref[rows, :].astype(full) + come_ref[rows, :].astype(full)).astype(half)


def norm_backward(a_ref, b_ref, c_ref, d_ref, stream_ref, cot_ref, grad_ref):
    upstream = (a_ref[...].astype(full) + c_ref[...].astype(full)) + (
        b_ref[...].astype(full) + d_ref[...].astype(full)
    )
    normed, inverse = centre(stream_ref[...])
    grad = cot_ref[...].astype(full) + inverse * (
        upstream
        - jnp.mean(upstream, axis=-1, keepdims=True)
        - normed * jnp.mean(upstream * normed, axis=-1, keepdims=True)
    )
    grad_ref[...] = grad.astype(half)


def merge(
    normed_ref,
    grad_ref,
    gated_ref,
    top_ref,
    error_in_ref,
    error_out_ref,
    factor_in_ref,
    factor_out_ref,
    merged_in_ref,
    merged_out_ref,
    left_ref,
    left_rows,
):
    merged_in = tn(normed_ref[...], grad_ref[...]).astype(half).astype(full) + error_in_ref[0]
    merged_in_ref[...] = merged_in
    left_ref[left_rows, :WIDTH] = left_product(factor_in_ref[0], merged_in).astype(half)
    merged_out = tn(gated_ref[...], top_ref[...]).astype(half).astype(full) + error_out_ref[0]
    merged_out_ref[...] = merged_out
    left_ref[left_rows, WIDTH:] = left_product(factor_out_ref[0], merged_out).astype(half)


def left_product(factor, merged):
    high, low = split(merged)
    factor_high, factor_low = split(factor)
    both = nt(jnp.concatenate([factor_high, factor_low], axis=0), high)
    return both[:RANK] + both[RANK:] + nt(factor_high, low)


def second_merge(
    normed_ref,
    grad_ref,
    gated_ref,
    cot_ref,
    error_in_ref,
    error_out_ref,
    factor_in_ref,
    factor_out_ref,
    merged_in_ref,
    merged_out_ref,
    left_ref,
):
    merge(
        normed_ref,
        grad_ref,
        gated_ref,
        cot_ref,
        error_in_ref,
        error_out_ref,
        factor_in_ref,
        factor_out_ref,
        merged_in_ref,
        merged_out_ref,
        left_ref,
        slice(0, RANK),
    )


def first_backward(device_ref, length_ref, table_ref, stamps_ref, proj_ref, normed_ref, *refs):
    blocks = refs[:8]
    weight_out_ref, error_in_ref, error_out_ref, factor_in_ref, factor_out_ref, other_ref = refs[8:14]
    merged_in_ref, merged_out_ref, left_ref = refs[14:17]
    top_ref, grad_ref, gated_ref, qa_ref, ka_ref, values_ref = refs[17:23]
    weights_ref, slope_ref, dk_ref, dv_ref = refs[23:]
    device = device_ref[0]
    for position, block in enumerate(blocks):
        top_ref[rows_of(device, position), :] = block[...]
    operands_from(proj_ref, stamps_ref, table_ref, qa_ref, ka_ref, values_ref)
    attend_backward(
        length_ref[0],
        qa_ref,
        ka_ref,
        values_ref,
        proj_ref,
        lambda rows: nt(top_ref[rows, :], weight_out_ref[...]),
        gated_ref,
        grad_ref,
        weights_ref,
        slope_ref,
        dk_ref,
        dv_ref,
    )
    left_ref[RANK:, :] = other_ref[...]
    merge(
        normed_ref,
        grad_ref,
        gated_ref,
        top_ref,
        error_in_ref,
        error_out_ref,
        factor_in_ref,
        factor_out_ref,
        merged_in_ref,
        merged_out_ref,
        left_ref,
        slice(0, RANK),
    )


def four_sum(a_ref, b_ref, c_ref, d_ref, rows, columns):
    return (a_ref[rows, columns].astype(full) + c_ref[rows, columns].astype(full)) + (
        b_ref[rows, columns].astype(full) + d_ref[rows, columns].astype(full)
    )


def ring_sum(a_ref, b_ref, c_ref, d_ref, out_ref):
    everything = slice(None)
    out_ref[...] = four_sum(a_ref, b_ref, c_ref, d_ref, everything, everything).astype(half)


def cholesky_inverses(grams):
    shape_ = (RANK, 2 * RANK)
    places = lax.broadcasted_iota(jnp.int32, shape_, 0)
    unit = jnp.where(
        lax.broadcasted_iota(jnp.int32, (RANK, RANK), 0)
        == lax.broadcasted_iota(jnp.int32, (RANK, RANK), 1),
        1.0,
        0.0,
    )
    work = [jnp.concatenate([gram, unit], axis=1) for gram in grams]
    for k in range(RANK):
        for m in range(len(work)):
            a = work[m]
            root = lax.rsqrt(a[k : k + 1, k : k + 1])
            row = a[k : k + 1, :] * root
            column = jnp.where(places > k, a[:, k : k + 1] * root, 0.0)
            work[m] = jnp.where(places == k, row, a - column * row)
    return [a[:, RANK:] for a in work]


def basis_right(*refs):
    sums = refs[:4]
    merged_refs = refs[4:8]
    basis_ref, right_ref = refs[8:]
    lefts = []
    for layer in range(2):
        rows = slice(layer * RANK, (layer + 1) * RANK)
        lefts.append(four_sum(*sums, rows, slice(0, WIDTH)))
        lefts.append(four_sum(*sums, rows, slice(WIDTH, WIDTH + HEAD)))
    inverses = cholesky_inverses([nt(left, left, highest) for left in lefts])
    for position in range(4):
        layer, out = divmod(position, 2)
        rows = slice(layer * RANK, (layer + 1) * RANK)
        columns = slice(WIDTH, WIDTH + HEAD) if out else slice(0, WIDTH)
        basis = jnp.dot(
            inverses[position], lefts[position], preferred_element_type=full, precision=highest
        )
        basis_ref[rows, columns] = basis
        high, low = split(merged_refs[position][...])
        basis_high, basis_low = split(basis)
        both = nn(jnp.concatenate([basis_high, basis_low], axis=0), high)
        right = both[:RANK] + both[RANK:] + nn(basis_high, low)
        columns = slice(WIDE, WIDE + WIDTH) if out else slice(0, WIDE)
        right_ref[rows, columns] = right.astype(half)


def finish(*refs):
    sums = refs[:4]
    basis_ref = refs[4]
    merged_refs = refs[5:9]
    update_in, update_out, next_in, next_out, error_in, error_out = refs[9:]
    for position in range(4):
        layer, out = divmod(position, 2)
        rows = slice(layer * RANK, (layer + 1) * RANK)
        columns = slice(WIDTH, WIDTH + HEAD) if out else slice(0, WIDTH)
        update_ref, next_ref, error_ref = (
            (update_out, next_out, error_out) if out else (update_in, next_in, error_in)
        )
        basis_high, basis_low = split(basis_ref[rows, columns])
        columns = slice(WIDE, WIDE + WIDTH) if out else slice(0, WIDE)
        right = four_sum(*sums, rows, columns) * (1.0 / 16)
        next_ref[layer] = right
        right_high, right_low = split(right)
        update = tn(
            jnp.concatenate([basis_high, basis_high, basis_low], axis=0),
            jnp.concatenate([right_high, right_low, right_high], axis=0),
        )
        update_ref[layer] = update
        error_ref[layer] = merged_refs[position][...] - update


def send_tp(x, chips):
    return lax.ppermute(x, "tp", [(k, (k - 2 * chips) % 8) for k in range(8)])


def swap(x):
    return lax.ppermute(x, "tp", [(k, k ^ 1) for k in range(8)])


def gather_tp(x):
    mine = [x] + [send_tp(x, chips) for chips in (1, 2, 3)]
    return mine + [swap(block) for block in mine]


def ring_z(x):
    return [x] + [
        lax.ppermute(x, "rep", [(k, k - k % 4 + (k - step) % 4) for k in range(16)])
        for step in (1, 2, 3)
    ]


def ring_x(x):
    return [x] + [
        lax.ppermute(x, "rep", [(k, (k - 4 * step) % 16) for k in range(16)]) for step in (1, 2, 3)
    ]


def sum_rep(x):
    parts = ring_z(x)
    part = call(
        ring_sum,
        "ring_sum",
        x.size * 4,
        x.size * 10,
        parts,
        [whole] * 4,
        [shape(x.shape, half)],
        [],
    )[0]
    return ring_x(part)


def layer_block(dims, layer):
    return pl.BlockSpec((1,) + dims, lambda step: (layer, 0, 0))


def per_device(
    inputs,
    cotangent,
    weight_in,
    weight_out,
    bias_table,
    lengths,
    stamps,
    factor_in,
    factor_out,
    error_in,
    error_out,
):
    device = lax.axis_index("tp").astype(jnp.int32).reshape(1)
    stamps = stamps.reshape(TOKENS, 1)
    weight_in = weight_in.reshape(2, WIDTH, WIDE)
    weight_out = weight_out.reshape(2, HEAD, WIDTH)
    factor_in = factor_in.reshape(2, RANK, WIDE)
    factor_out = factor_out.reshape(2, RANK, WIDTH)
    error_in = error_in.reshape(2, WIDTH, WIDE)
    error_out = error_out.reshape(2, HEAD, WIDTH)

    input_blocks = gather_tp(inputs)
    mix_all = lax.all_gather(weight_out[0], "tp", axis=0, tiled=True)
    cot_all = lax.all_gather(cotangent, "tp", axis=0, tiled=True)

    attention_scratch = [
        pltpu.VMEM((TOKENS, 2 * HEAD), half),
        pltpu.VMEM((TOKENS, 2 * HEAD), half),
        pltpu.VMEM((TOKENS, HEAD), half),
    ]
    backward_scratch = [
        pltpu.VMEM((BLOCK, TOKENS), half),
        pltpu.VMEM((BLOCK, TOKENS), full),
        pltpu.VMEM((TOKENS, HEAD), full),
        pltpu.VMEM((TOKENS, HEAD), full),
    ]
    dot_flops = 2 * TOKENS * WIDTH * WIDE

    rows_all, normed_0, proj_0, gated_0 = call(
        first_forward,
        "first_forward",
        3 * dot_flops,
        12 << 20,
        (device, lengths, bias_table[0], stamps, *input_blocks, weight_in[0]),
        [scalars] * 3 + [whole] * 10,
        [
            shape((TOKENS, WIDTH), half),
            shape((TOKENS, WIDTH), half),
            shape((TOKENS, WIDE), full),
            shape((TOKENS, HEAD), half),
        ],
        attention_scratch,
    )
    gated_blocks = gather_tp(gated_0)

    normed_1, grad_1, gated_1, send, keep, stream = call(
        second_layer,
        "second_layer",
        10 * dot_flops,
        18 << 20,
        (
            device,
            lengths,
            bias_table[1],
            stamps,
            rows_all,
            *gated_blocks,
            mix_all,
            weight_in[1],
            cot_all,
            weight_out[1],
        ),
        [scalars] * 3 + [whole] * 14,
        [
            shape((TOKENS, WIDTH), half),
            shape((TOKENS, WIDE), half),
            shape((TOKENS, HEAD), half),
            shape((TOKENS // 2, WIDTH), half),
            shape((TOKENS // 2, WIDTH), half),
            shape((OWN, WIDTH), full),
        ],
        [
            pltpu.VMEM((TOKENS, WIDTH), half),
            pltpu.VMEM((TOKENS, WIDE), full),
            *attention_scratch,
            *backward_scratch,
            pltpu.VMEM((TOKENS, WIDTH), full),
        ],
    )
    come = swap(send)
    sums = call(
        pair_sum,
        "pair_sum",
        TOKENS * WIDTH,
        3 << 20,
        (keep, come),
        [whole] * 2,
        [shape((OWN, WIDTH), half)] * 4,
        [],
    )
    parts = [sums[0]] + [
        lax.ppermute(sums[chips], "tp", [(k, (k + 2 * chips) % 8) for k in range(8)])
        for chips in (1, 2, 3)
    ]
    grad_own = call(
        norm_backward,
        "norm_backward",
        OWN * WIDTH * 20,
        2 << 20,
        (*parts, stream, cotangent),
        [whole] * 6,
        [shape((OWN, WIDTH), half)],
        [],
    )[0]
    grad_blocks = gather_tp(grad_own)

    merge_specs = [
        (layer_block((WIDTH, WIDE), layer), layer_block((HEAD, WIDTH), layer))
        + (layer_block((RANK, WIDE), layer), layer_block((RANK, WIDTH), layer))
        for layer in range(2)
    ]
    merged_shapes = [shape((WIDTH, WIDE), full), shape((HEAD, WIDTH), full)]
    merged_in_1, merged_out_1, left_1 = call(
        second_merge,
        "second_merge",
        3 * dot_flops,
        12 << 20,
        (normed_1, grad_1, gated_1, cot_all, error_in, error_out, factor_in, factor_out),
        [whole] * 4 + list(merge_specs[1]),
        merged_shapes + [shape((RANK, WIDTH + HEAD), half)],
        [],
    )
    merged_in_0, merged_out_0, left = call(
        first_backward,
        "first_backward",
        8 * dot_flops,
        18 << 20,
        (
            device,
            lengths,
            bias_table[0],
            stamps,
            proj_0,
            normed_0,
            *grad_blocks,
            weight_out[0],
            error_in,
            error_out,
            factor_in,
            factor_out,
            left_1,
        ),
        [scalars] * 3 + [whole] * 12 + list(merge_specs[0]) + [whole],
        merged_shapes + [shape((2 * RANK, WIDTH + HEAD), half)],
        [
            pltpu.VMEM((TOKENS, WIDTH), half),
            pltpu.VMEM((TOKENS, WIDE), half),
            pltpu.VMEM((TOKENS, HEAD), half),
            *attention_scratch,
            *backward_scratch,
        ],
    )
    merged = (merged_in_0, merged_out_0, merged_in_1, merged_out_1)
    basis, right = call(
        basis_right,
        "basis_right",
        dot_flops,
        8 << 20,
        (*sum_rep(left), *merged),
        [whole] * 8,
        [shape((2 * RANK, WIDTH + HEAD), full), shape((2 * RANK, WIDE + WIDTH), half)],
        [],
    )
    outs = call(
        finish,
        "finish",
        dot_flops,
        16 << 20,
        (*sum_rep(right), basis, *merged),
        [whole] * 9,
        [
            shape((2, WIDTH, WIDE), full),
            shape((2, HEAD, WIDTH), full),
            shape((2, RANK, WIDE), full),
            shape((2, RANK, WIDTH), full),
            shape((2, WIDTH, WIDE), full),
            shape((2, HEAD, WIDTH), full),
        ],
        [],
    )
    update_in, update_out, next_in, next_out, error_in_next, error_out_next = outs
    return (
        update_in.reshape(2, 1, WIDTH, WIDE),
        update_out.reshape(2, 1, HEAD, WIDTH),
        next_in.reshape(2, 1, RANK, WIDE),
        next_out.reshape(2, 1, RANK, WIDTH),
        error_in_next.reshape(1, 2, 1, WIDTH, WIDE),
        error_out_next.reshape(1, 2, 1, HEAD, WIDTH),
    )


def solution(mesh):
    placed_in = (
        P(("rep", "tp"), None),
        P(("rep", "tp"), None),
        P(None, None, None, "tp", None),
        P(None, "tp", None, None),
        P(None, "tp", None),
        P("rep"),
        P("rep", None),
        P(None, "tp", None, None),
        P(None, "tp", None, None),
        P("rep", None, "tp", None, None),
        P("rep", None, "tp", None, None),
    )
    return jax.shard_map(
        per_device,
        mesh=mesh,
        in_specs=placed_in,
        out_specs=(
            P(None, "tp", None, None),
            P(None, "tp", None, None),
            P(None, "tp", None, None),
            P(None, "tp", None, None),
            P("rep", None, "tp", None, None),
            P("rep", None, "tp", None, None),
        ),
        check_vma=False,
    )
```

```python
import functools

import jax
import jax.numpy as jnp
from jax import lax
from jax.experimental import pallas as pl
from jax.experimental.pallas import tpu as pltpu
from jax.sharding import PartitionSpec as P

epsilon = 1e-05
highest = lax.Precision.HIGHEST
half = jnp.bfloat16
full = jnp.float32

TOKENS = 1024
WIDTH = 1024
HEAD = 128
WIDE = 4 * HEAD
RANK = 32
BUCKETS = 16
OWN = 128
BLOCK = 256
BLOCKS = TOKENS // BLOCK
MESSAGE = TOKENS + 16
SPARE_BYTES = 8 * 1024 * 1024

whole = pl.BlockSpec(memory_space=pltpu.VMEM)
scalars = pl.BlockSpec(memory_space=pltpu.SMEM)


def nn(a, b):
    return jnp.dot(a, b, preferred_element_type=full)


def nt(a, b, precision=None):
    return lax.dot_general(
        a, b, (((1,), (1,)), ((), ())), preferred_element_type=full, precision=precision
    )


def tn(a, b, precision=None):
    return lax.dot_general(
        a, b, (((0,), (0,)), ((), ())), preferred_element_type=full, precision=precision
    )


def logistic(x):
    return 0.5 * jnp.tanh(0.5 * x) + 0.5


def silu_slope(x):
    s = logistic(x)
    return s * (1.0 + x * (1.0 - s))


def centre(x):
    c = x - jnp.mean(x, axis=-1, keepdims=True)
    inverse = lax.rsqrt(jnp.mean(c * c, axis=-1, keepdims=True) + epsilon)
    return c * inverse, inverse


def split(x):
    high = x.astype(half)
    return high, (x - high.astype(full)).astype(half)


def room(dims, dtype):
    lanes = -(-dims[-1] // 128) * 128
    rows = 1
    for extent in dims[:-1]:
        rows *= extent
    return max(rows, 8) * lanes * jnp.dtype(dtype).itemsize


def call(body, name, flops, operands, in_specs, outs, scratch, out_specs=None, aliases=None):
    specs = list(in_specs) + list(out_specs or [])
    grid = {} if all(spec.block_shape is None for spec in specs) else {"grid": (1,)}
    buffers = [
        (spec.block_shape or operand.shape, operand.dtype)
        for spec, operand in zip(in_specs, operands)
        if spec.memory_space is not pl.ANY
    ]
    buffers += [
        (spec.block_shape or out.shape, out.dtype)
        for spec, out in zip(out_specs or [whole] * len(outs), outs)
    ]
    held = sum(room(*buffer) for buffer in buffers)
    moved = sum(out.size * out.dtype.itemsize for out in list(operands) + list(outs))
    return pl.pallas_call(
        body,
        name=name,
        **grid,
        out_shape=outs,
        in_specs=in_specs,
        out_specs=out_specs if out_specs is not None else [whole] * len(outs),
        scratch_shapes=scratch,
        input_output_aliases=aliases or {},
        compiler_params=pltpu.CompilerParams(
            vmem_limit_bytes=held * (2 if grid else 1)
            + sum(room(piece.shape, piece.dtype) for piece in scratch)
            + SPARE_BYTES
        ),
        cost_estimate=pl.CostEstimate(flops=flops, bytes_accessed=moved, transcendentals=0),
    )(*operands)


def shape(dims, dtype):
    return jax.ShapeDtypeStruct(dims, dtype)


def placed(device, position):
    core = lax.rem(device, 2)
    base = device if position < 4 else device + 1 - 2 * core
    way = 2 * core - 1 if position < 4 else 1 - 2 * core
    return lax.rem(base + (0, 2 * way, -2 * way, 4)[position % 4] + 8, 8)


def rows_of(device, position):
    return pl.ds(pl.multiple_of(placed(device, position) * OWN, OWN), OWN)


def attention_operands(stamps_ref, table_ref, query_of, key_of, qa_ref, ka_ref):
    scale = HEAD**-0.5
    places = lax.broadcasted_iota(jnp.int32, (HEAD, HEAD), 0)
    lanes = lax.broadcasted_iota(jnp.int32, (HEAD, HEAD), 1)
    gap = jnp.clip(places - (lanes & 63), 0, BUCKETS - 1)
    lookup = jnp.zeros((HEAD, HEAD), full)
    for bucket in range(BUCKETS):
        lookup = jnp.where(gap == bucket, table_ref[0, bucket] * (1.0 / scale), lookup)
    high = lookup.astype(half).astype(full)
    lookup = jnp.where(lanes < 64, high, lookup - high)
    lookup = jnp.where(places < 64, lookup, 0.0).astype(half)
    first = stamps_ref[0:1, :]
    for part in range(BLOCKS):
        rows = slice(part * BLOCK, (part + 1) * BLOCK)
        since = stamps_ref[rows, :] - first
        columns = lax.broadcasted_iota(jnp.int32, (BLOCK, HEAD), 1)
        hot = jnp.where(since == (columns & 63), 1.0, 0.0)
        left_hot = jnp.where(columns < 64, hot, 0.0).astype(half)
        qa_ref[rows, HEAD:] = nn(left_hot, lookup).astype(half)
        ka_ref[rows, HEAD:] = hot.astype(half)
        qa_ref[rows, :HEAD] = query_of(rows)
        ka_ref[rows, :HEAD] = key_of(rows)


def score_block(qa_ref, ka_ref, i, j):
    return nt(
        qa_ref[i * BLOCK : (i + 1) * BLOCK, :], ka_ref[j * BLOCK : (j + 1) * BLOCK, :]
    ) * (HEAD**-0.5)


def causal():
    return lax.broadcasted_iota(jnp.int32, (BLOCK, BLOCK), 0) >= lax.broadcasted_iota(
        jnp.int32, (BLOCK, BLOCK), 1
    )


def row_mask(i, length):
    places = lax.broadcasted_iota(jnp.int32, (BLOCK, HEAD), 0) + i * BLOCK
    return places < length


def attend_forward(length, qa_ref, ka_ref, values_ref, proj_ref, gated_ref):
    share = 1.0 / length.astype(full)
    for i in range(BLOCKS):
        rows = slice(i * BLOCK, (i + 1) * BLOCK)
        total = jnp.zeros((BLOCK, HEAD), full)
        for j in range(i + 1):
            s = score_block(qa_ref, ka_ref, i, j)
            w = s * logistic(s)
            if i == j:
                w = jnp.where(causal(), w, 0.0)
            total += nn(w.astype(half), values_ref[j * BLOCK : (j + 1) * BLOCK, :])
        attended = jnp.where(row_mask(i, length), total * share, 0.0)
        normed, _ = centre(attended)
        gate = proj_ref[rows, :HEAD]
        gate = (gate * logistic(gate)).astype(half).astype(full)
        gated_ref[rows, :] = (normed * gate).astype(half)


def attend_backward(
    length,
    qa_ref,
    ka_ref,
    values_ref,
    proj_ref,
    upstream_of,
    gated_ref,
    grad_ref,
    weights_ref,
    slope_ref,
    dk_ref,
    dv_ref,
):
    share = 1.0 / length.astype(full)
    scale = HEAD**-0.5
    for i in range(BLOCKS):
        rows = slice(i * BLOCK, (i + 1) * BLOCK)
        total = jnp.zeros((BLOCK, HEAD), full)
        for j in range(i + 1):
            cols = slice(j * BLOCK, (j + 1) * BLOCK)
            s = score_block(qa_ref, ka_ref, i, j)
            sigmoid = logistic(s)
            w = s * sigmoid
            slope = sigmoid + w * (1.0 - sigmoid)
            if i == j:
                w = jnp.where(causal(), w, 0.0)
                slope = jnp.where(causal(), slope, 0.0)
            w = w.astype(half)
            weights_ref[:, cols] = w
            slope_ref[:, cols] = slope
            total += nn(w, values_ref[cols, :])
        inside = row_mask(i, length)
        attended = jnp.where(inside, total * share, 0.0)
        normed, inverse = centre(attended)
        gate_raw = proj_ref[rows, :HEAD]
        gate = (gate_raw * logistic(gate_raw)).astype(half).astype(full)
        gated_ref[rows, :] = (normed * gate).astype(half)
        upstream = upstream_of(rows)
        grad_ref[rows, :HEAD] = (upstream * normed * silu_slope(gate_raw)).astype(half)
        g = upstream * gate
        back = inverse * (
            g
            - jnp.mean(g, axis=-1, keepdims=True)
            - normed * jnp.mean(g * normed, axis=-1, keepdims=True)
        )
        back = jnp.where(inside, back, 0.0).astype(half)
        dq = jnp.zeros((BLOCK, HEAD), full)
        for j in range(i + 1):
            cols = slice(j * BLOCK, (j + 1) * BLOCK)
            ds = (nt(back, values_ref[cols, :]) * slope_ref[:, cols]).astype(half)
            dq += nn(ds, ka_ref[cols, :HEAD])
            dk = tn(ds, qa_ref[rows, :HEAD])
            dv = tn(weights_ref[:, cols], back)
            if i == j:
                dk_ref[cols, :] = dk
                dv_ref[cols, :] = dv
            else:
                dk_ref[cols, :] += dk
                dv_ref[cols, :] += dv
        raw = proj_ref[rows, 2 * HEAD : 3 * HEAD]
        grad_ref[rows, 2 * HEAD : 3 * HEAD] = (dq * (scale * share) * silu_slope(raw)).astype(half)
    for i in range(BLOCKS):
        rows = slice(i * BLOCK, (i + 1) * BLOCK)
        raw = proj_ref[rows, HEAD : 2 * HEAD]
        grad_ref[rows, HEAD : 2 * HEAD] = (dv_ref[rows, :] * share * silu_slope(raw)).astype(half)
        raw = proj_ref[rows, 3 * HEAD :]
        grad_ref[rows, 3 * HEAD :] = (dk_ref[rows, :] * (scale * share) * silu_slope(raw)).astype(
            half
        )


def silu_half(x):
    return (x * logistic(x)).astype(half)


def operands_from(proj_ref, stamps_ref, table_ref, qa_ref, ka_ref, values_ref):
    attention_operands(
        stamps_ref,
        table_ref,
        lambda rows: silu_half(proj_ref[rows, 2 * HEAD : 3 * HEAD]),
        lambda rows: silu_half(proj_ref[rows, 3 * HEAD :]),
        qa_ref,
        ka_ref,
    )
    for part in range(BLOCKS):
        rows = slice(part * BLOCK, (part + 1) * BLOCK)
        values_ref[rows, :] = silu_half(proj_ref[rows, HEAD : 2 * HEAD])


def first_forward(device_ref, length_ref, table_ref, stamps_ref, *refs):
    blocks = refs[:8]
    weight_ref, rows_ref, normed_ref, proj_ref, gated_ref, qa_ref, ka_ref, values_ref = refs[8:]
    device = device_ref[0]
    for position, block in enumerate(blocks):
        rows_ref[rows_of(device, position), :] = block[...]
    for part in range(BLOCKS):
        rows = slice(part * BLOCK, (part + 1) * BLOCK)
        normed = centre(rows_ref[rows, :].astype(full))[0].astype(half)
        normed_ref[rows, :] = normed
        proj_ref[rows, :] = nn(normed, weight_ref[...])
    operands_from(proj_ref, stamps_ref, table_ref, qa_ref, ka_ref, values_ref)
    attend_forward(length_ref[0], qa_ref, ka_ref, values_ref, proj_ref, gated_ref)


def products(device_ref, *refs):
    blocks = refs[:8]
    weight_ref, mix_ref, cot_ref, product_ref = refs[8:]
    device = device_ref[0]
    for position, block in enumerate(blocks):
        mix_ref[position * HEAD : (position + 1) * HEAD, :] = block[:HEAD, :]
        cot_ref[rows_of(device, position), :] = block[HEAD:, :]
    for part in range(BLOCKS):
        rows = slice(part * BLOCK, (part + 1) * BLOCK)
        product_ref[rows, :] = nn(mix_ref[rows, :], weight_ref[...]).astype(half)


def second_layer(length_ref, table_ref, stamps_ref, rows_ref, *refs):
    heads = refs[:8]
    mix_ref, weight_in_ref, cot_ref, weight_out_ref, product_ref = refs[8:13]
    normed_ref, grad_ref, scaled_ref, gated_ref, send_ref, keep_ref = refs[13:19]
    all_ref, proj_ref, qa_ref, ka_ref, values_ref = refs[19:24]
    weights_ref, slope_ref, dk_ref, dv_ref, inverse_ref, sums_ref = refs[24:]
    for position, block in enumerate(heads):
        all_ref[:, position * HEAD : (position + 1) * HEAD] = block[...]
    for part in range(BLOCKS):
        rows = slice(part * BLOCK, (part + 1) * BLOCK)
        stream = rows_ref[rows, :].astype(full) + nn(all_ref[rows, :], mix_ref[...])
        normed, inverse = centre(stream)
        normed = normed.astype(half)
        normed_ref[rows, :] = normed
        inverse_ref[rows, :] = jnp.broadcast_to(inverse, (BLOCK, HEAD))
        proj_ref[rows, :] = nn(normed, weight_in_ref[...])
    operands_from(proj_ref, stamps_ref, table_ref, qa_ref, ka_ref, values_ref)
    attend_backward(
        length_ref[0],
        qa_ref,
        ka_ref,
        values_ref,
        proj_ref,
        lambda rows: nt(cot_ref[rows, :], weight_out_ref[...]),
        gated_ref,
        grad_ref,
        weights_ref,
        slope_ref,
        dk_ref,
        dv_ref,
    )
    ones = jnp.ones((16, WIDTH), half)
    column_sum = nn(ones, weight_in_ref[...])
    high = column_sum.astype(half).astype(full)
    places = lax.broadcasted_iota(jnp.int32, (16, WIDE), 0)
    column_sum = jnp.where(
        places == 0, high, jnp.where(places == 1, column_sum - high, 0.0)
    ).astype(half)
    for part in range(BLOCKS):
        rows = slice(part * BLOCK, (part + 1) * BLOCK)
        for piece in range(4):
            lanes = slice(piece * HEAD, (piece + 1) * HEAD)
            scaled_ref[rows, lanes] = (
                grad_ref[rows, lanes].astype(full) * inverse_ref[rows, :]
            ).astype(half)
        scaled = scaled_ref[rows, :]
        by_head = nt(scaled, product_ref[...]).astype(half)
        for position in range(4):
            out = slice(position * MESSAGE + part * BLOCK, position * MESSAGE + (part + 1) * BLOCK)
            keep_ref[out, :] = by_head[:, position * HEAD : (position + 1) * HEAD]
            send_ref[out, :] = by_head[:, (position + 4) * HEAD : (position + 5) * HEAD]
        sums = nt(column_sum, scaled)
        first = sums[0:1, :] + sums[1:2, :]
        high, low = split(scaled.astype(full) * proj_ref[rows, :])
        second = (nt(ones[:, :WIDE], high) + nt(ones[:, :WIDE], low))[0:1, :]
        for piece in range(BLOCK // HEAD):
            lanes = slice(piece * HEAD, (piece + 1) * HEAD)
            row = part * (BLOCK // HEAD) + piece
            sums_ref[row : row + 1, :] = first[:, lanes]
            sums_ref[8 + row : 9 + row, :] = second[:, lanes]
    sums = sums_ref[...].astype(half)
    for position in range(4):
        out = slice(position * MESSAGE + TOKENS, (position + 1) * MESSAGE)
        keep_ref[out, :] = sums
        send_ref[out, :] = sums


def out_partials(*refs):
    heads = refs[:8]
    scaled_ref, weight_ref, send_ref, keep_ref = refs[8:]
    for position, block in enumerate(heads):
        inner = tn(block[...], scaled_ref[...]).astype(half)
        out_ref = keep_ref if position < 4 else send_ref
        out = slice(position % 4 * HEAD, (position % 4 + 1) * HEAD)
        out_ref[out, :] = nt(inner, weight_ref[...]).astype(half)


def pair_sum(keep_ref, come_ref, *outs):
    extent = keep_ref.shape[0] // 4
    for position, out in enumerate(outs):
        rows = slice(position * extent, (position + 1) * extent)
        out[...] = (keep_ref[rows, :].astype(full) + come_ref[rows, :].astype(full)).astype(half)


def left_product(factor, merged):
    high, low = split(merged)
    factor_high, factor_low = split(factor)
    both = nt(jnp.concatenate([factor_high, factor_low], axis=0), high)
    return both[:RANK] + both[RANK:] + nt(factor_high, low)


def second_merge(
    normed_ref,
    grad_ref,
    gated_ref,
    cot_ref,
    error_in_ref,
    error_out_ref,
    factor_in_ref,
    factor_out_ref,
    merged_in_ref,
    merged_out_ref,
    left_ref,
):
    merged_in = tn(normed_ref[...], grad_ref[...]).astype(half).astype(full) + error_in_ref[0]
    merged_in_ref[...] = merged_in
    left_ref[:, :WIDTH] = left_product(factor_in_ref[0], merged_in).astype(half)
    merged_out = tn(gated_ref[...], cot_ref[...]).astype(half).astype(full) + error_out_ref[0]
    merged_out_ref[...] = merged_out
    left_ref[:, WIDTH:] = left_product(factor_out_ref[0], merged_out).astype(half)


def first_backward(length_ref, table_ref, stamps_ref, proj_ref, normed_ref, above_ref, cot_ref, *refs):
    parts = refs[:4]
    weight_out_ref, error_in_ref, factor_in_ref = refs[4:7]
    merged_in_ref, left_ref, top_ref = refs[7:10]
    grad_ref, gated_ref, qa_ref, ka_ref, values_ref = refs[10:15]
    weights_ref, slope_ref, dk_ref, dv_ref = refs[15:]
    sums = four_sum(*parts, slice(TOKENS, MESSAGE), slice(None)) * (1.0 / WIDTH)
    high = sums.astype(half).astype(full)
    ones = jnp.ones((16, HEAD), half)
    places = lax.broadcasted_iota(jnp.int32, (16, HEAD), 0)
    for part in range(TOKENS // OWN):
        rows = slice(part * OWN, (part + 1) * OWN)
        both = []
        for row in (part, 8 + part):
            spread = jnp.where(
                places == 0, high[row : row + 1, :], jnp.where(places == 1, (sums - high)[row : row + 1, :], 0.0)
            ).astype(half)
            both.append(tn(spread, ones))
        for piece in range(WIDTH // HEAD):
            lanes = slice(piece * HEAD, (piece + 1) * HEAD)
            top_ref[rows, lanes] = (
                cot_ref[rows, lanes].astype(full)
                - (both[0] + both[1] * above_ref[rows, lanes].astype(full))
            ).astype(half)
    operands_from(proj_ref, stamps_ref, table_ref, qa_ref, ka_ref, values_ref)
    attend_backward(
        length_ref[0],
        qa_ref,
        ka_ref,
        values_ref,
        proj_ref,
        lambda rows: nt(top_ref[rows, :], weight_out_ref[...]) + four_sum(*parts, rows, slice(None)),
        gated_ref,
        grad_ref,
        weights_ref,
        slope_ref,
        dk_ref,
        dv_ref,
    )
    merged_in = tn(normed_ref[...], grad_ref[...]).astype(half).astype(full) + error_in_ref[0]
    merged_in_ref[...] = merged_in
    left_ref[...] = left_product(factor_in_ref[0], merged_in).astype(half)


def first_merge(gated_ref, top_ref, a_ref, b_ref, c_ref, d_ref, error_ref, factor_ref, left_in_ref, *outs):
    merged_ref, left_ref = outs
    everything = slice(None)
    grad = tn(gated_ref[...], top_ref[...]) + four_sum(
        a_ref, b_ref, c_ref, d_ref, everything, everything
    )
    merged = grad.astype(half).astype(full) + error_ref[0]
    merged_ref[...] = merged
    left_ref[:, :WIDTH] = left_in_ref[...]
    left_ref[:, WIDTH:] = left_product(factor_ref[0], merged).astype(half)


def four_sum(a_ref, b_ref, c_ref, d_ref, rows, columns):
    return (a_ref[rows, columns].astype(full) + c_ref[rows, columns].astype(full)) + (
        b_ref[rows, columns].astype(full) + d_ref[rows, columns].astype(full)
    )


def ring_sum(a_ref, b_ref, c_ref, d_ref, out_ref):
    everything = slice(None)
    out_ref[...] = four_sum(a_ref, b_ref, c_ref, d_ref, everything, everything).astype(half)


def cholesky_inverses(grams):
    shape_ = (RANK, 2 * RANK)
    places = lax.broadcasted_iota(jnp.int32, shape_, 0)
    unit = jnp.where(
        lax.broadcasted_iota(jnp.int32, (RANK, RANK), 0)
        == lax.broadcasted_iota(jnp.int32, (RANK, RANK), 1),
        1.0,
        0.0,
    )
    work = [jnp.concatenate([gram, unit], axis=1) for gram in grams]
    for k in range(RANK):
        for m in range(len(work)):
            a = work[m]
            root = lax.rsqrt(a[k : k + 1, k : k + 1])
            row = a[k : k + 1, :] * root
            column = jnp.where(places > k, a[:, k : k + 1] * root, 0.0)
            work[m] = jnp.where(places == k, row, a - column * row)
    return [a[:, RANK:] for a in work]


def basis_right(*refs):
    sums = refs[:4]
    merged_refs = refs[4:6]
    basis_ref, right_ref = refs[6:]
    columns = (slice(0, WIDTH), slice(WIDTH, WIDTH + HEAD))
    places = (slice(0, WIDE), slice(WIDE, WIDE + WIDTH))
    lefts = [four_sum(*sums, slice(None), column) for column in columns]
    inverses = cholesky_inverses([nt(left, left, highest) for left in lefts])
    for out in range(2):
        basis = jnp.dot(inverses[out], lefts[out], preferred_element_type=full, precision=highest)
        basis_ref[:, columns[out]] = basis
        high, low = split(merged_refs[out][...])
        basis_high, basis_low = split(basis)
        both = nn(jnp.concatenate([basis_high, basis_low], axis=0), high)
        right = both[:RANK] + both[RANK:] + nn(basis_high, low)
        right_ref[:, places[out]] = right.astype(half)


def finish(*refs):
    sums = refs[:4]
    basis_ref = refs[4]
    merged_refs = refs[5:7]
    update_in, update_out, next_in, next_out, error_in, error_out = refs[-6:]
    columns = (slice(0, WIDTH), slice(WIDTH, WIDTH + HEAD))
    places = (slice(0, WIDE), slice(WIDE, WIDE + WIDTH))
    for out in range(2):
        update_ref, next_ref, error_ref = (
            (update_out, next_out, error_out) if out else (update_in, next_in, error_in)
        )
        basis_high, basis_low = split(basis_ref[:, columns[out]])
        right = four_sum(*sums, slice(None), places[out]) * (1.0 / 16)
        next_ref[0] = right
        right_high, right_low = split(right)
        update = tn(
            jnp.concatenate([basis_high, basis_high, basis_low], axis=0),
            jnp.concatenate([right_high, right_low, right_high], axis=0),
        )
        update_ref[0] = update
        error_ref[0] = merged_refs[out][...] - update


def swap(x):
    return lax.ppermute(x, "tp", [(k, k ^ 1) for k in range(8)])


def first_way(x):
    return lax.ppermute(x, "tp", [(k, (k + 2 - 4 * (k % 2)) % 8) for k in range(8)])


def other_way(x):
    return lax.ppermute(x, "tp", [(k, (k - 2 + 4 * (k % 2)) % 8) for k in range(8)])


def across(x):
    return lax.ppermute(x, "tp", [(k, (k + 4) % 8) for k in range(8)])


def gather_tp(x):
    near = first_way(x)
    mine = [x, near, other_way(x), first_way(near)]
    return mine + [swap(block) for block in mine]


def scatter_tp(send, keep, name):
    extent = (keep.shape[0] // 4, keep.shape[1])
    sums = call(
        pair_sum,
        name,
        keep.size,
        (keep, swap(send)),
        [whole] * 2,
        [shape(extent, half)] * 4,
        [],
    )
    return [sums[0], other_way(sums[1]), across(sums[3]), first_way(sums[2])]


def ring_z(x):
    return [x] + [
        lax.ppermute(x, "rep", [(k, k - k % 4 + (k - step) % 4) for k in range(16)])
        for step in (1, 2, 3)
    ]


def ring_x(x):
    return [x] + [
        lax.ppermute(x, "rep", [(k, (k - 4 * step) % 16) for k in range(16)]) for step in (1, 2, 3)
    ]


def sum_rep(x, name):
    parts = ring_z(x)
    part = call(ring_sum, name, x.size * 4, parts, [whole] * 4, [shape(x.shape, half)], [])[0]
    return ring_x(part)


def compress(left, merged, layer, others):
    basis, right = call(
        basis_right,
        f"basis_right_{layer}",
        TOKENS * WIDTH * WIDE // 4,
        (*sum_rep(left, f"left_sum_{layer}"), *merged),
        [whole] * 6,
        [shape((RANK, WIDTH + HEAD), full), shape((RANK, WIDE + WIDTH), half)],
        [],
    )
    blocks = [(WIDTH, WIDE), (HEAD, WIDTH), (RANK, WIDE), (RANK, WIDTH), (WIDTH, WIDE), (HEAD, WIDTH)]
    return call(
        finish,
        f"finish_{layer}",
        TOKENS * WIDTH * WIDE // 4,
        (*sum_rep(right, f"right_sum_{layer}"), basis, *merged, *others),
        [whole] * 7 + [pl.BlockSpec(memory_space=pl.ANY)] * len(others),
        [shape((2,) + block, full) for block in blocks],
        [],
        [layer_block(block, layer) for block in blocks],
        {7 + position: position for position in range(len(others))},
    )


def layer_block(dims, layer):
    return pl.BlockSpec((1,) + dims, lambda step: (layer, 0, 0))


def per_device(
    inputs,
    cotangent,
    weight_in,
    weight_out,
    bias_table,
    lengths,
    stamps,
    factor_in,
    factor_out,
    error_in,
    error_out,
):
    device = lax.axis_index("tp").astype(jnp.int32).reshape(1)
    stamps = stamps.reshape(TOKENS, 1)
    weight_in = weight_in.reshape(2, WIDTH, WIDE)
    weight_out = weight_out.reshape(2, HEAD, WIDTH)
    factor_in = factor_in.reshape(2, RANK, WIDE)
    factor_out = factor_out.reshape(2, RANK, WIDTH)
    error_in = error_in.reshape(2, WIDTH, WIDE)
    error_out = error_out.reshape(2, HEAD, WIDTH)

    input_blocks = gather_tp(inputs)
    early_blocks = gather_tp(jnp.concatenate([weight_out[0], cotangent], axis=0))

    attention_scratch = [
        pltpu.VMEM((TOKENS, 2 * HEAD), half),
        pltpu.VMEM((TOKENS, 2 * HEAD), half),
        pltpu.VMEM((TOKENS, HEAD), half),
    ]
    backward_scratch = [
        pltpu.VMEM((BLOCK, TOKENS), half),
        pltpu.VMEM((BLOCK, TOKENS), full),
        pltpu.VMEM((TOKENS, HEAD), full),
        pltpu.VMEM((TOKENS, HEAD), full),
    ]
    dot_flops = 2 * TOKENS * WIDTH * WIDE

    rows_all, normed_0, proj_0, gated_0 = call(
        first_forward,
        "first_forward",
        3 * dot_flops,
        (device, lengths, bias_table[0], stamps, *input_blocks, weight_in[0]),
        [scalars] * 3 + [whole] * 10,
        [
            shape((TOKENS, WIDTH), half),
            shape((TOKENS, WIDTH), half),
            shape((TOKENS, WIDE), full),
            shape((TOKENS, HEAD), half),
        ],
        attention_scratch,
    )
    mix_all, cot_all, product = call(
        products,
        "products",
        dot_flops,
        (device, *early_blocks, weight_in[1]),
        [scalars] + [whole] * 9,
        [shape((TOKENS, WIDTH), half), shape((TOKENS, WIDTH), half), shape((WIDTH, WIDE), half)],
        [],
    )
    gated_blocks = gather_tp(gated_0)

    message = shape((4 * MESSAGE, HEAD), half)
    normed_1, grad_1, scaled_1, gated_1, send, keep = call(
        second_layer,
        "second_layer",
        10 * dot_flops,
        (
            lengths,
            bias_table[1],
            stamps,
            rows_all,
            *gated_blocks,
            mix_all,
            weight_in[1],
            cot_all,
            weight_out[1],
            product,
        ),
        [scalars] * 2 + [whole] * 15,
        [
            shape((TOKENS, WIDTH), half),
            shape((TOKENS, WIDE), half),
            shape((TOKENS, WIDE), half),
            shape((TOKENS, HEAD), half),
            message,
            message,
        ],
        [
            pltpu.VMEM((TOKENS, WIDTH), half),
            pltpu.VMEM((TOKENS, WIDE), full),
            *attention_scratch,
            *backward_scratch,
            pltpu.VMEM((TOKENS, HEAD), full),
            pltpu.VMEM((16, HEAD), full),
        ],
    )
    gated_parts = scatter_tp(send, keep, "gated_pairs")
    out_send, out_keep = call(
        out_partials,
        "out_partials",
        2 * dot_flops,
        (*gated_blocks, scaled_1, weight_in[1]),
        [whole] * 10,
        [shape((4 * HEAD, WIDTH), half)] * 2,
        [],
    )
    out_parts = scatter_tp(out_send, out_keep, "out_pairs")

    merged_shapes = [shape((WIDTH, WIDE), full), shape((HEAD, WIDTH), full)]
    merged_in_1, merged_out_1, left_1 = call(
        second_merge,
        "second_merge",
        3 * dot_flops,
        (normed_1, grad_1, gated_1, cot_all, error_in, error_out, factor_in, factor_out),
        [whole] * 4
        + [
            layer_block((WIDTH, WIDE), 1),
            layer_block((HEAD, WIDTH), 1),
            layer_block((RANK, WIDE), 1),
            layer_block((RANK, WIDTH), 1),
        ],
        merged_shapes + [shape((RANK, WIDTH + HEAD), half)],
        [],
        [whole] * 3,
    )
    merged_in_0, left_in_0, top = call(
        first_backward,
        "first_backward",
        8 * dot_flops,
        (
            lengths,
            bias_table[0],
            stamps,
            proj_0,
            normed_0,
            normed_1,
            cot_all,
            *gated_parts,
            weight_out[0],
            error_in,
            factor_in,
        ),
        [scalars] * 2
        + [whole] * 10
        + [layer_block((WIDTH, WIDE), 0), layer_block((RANK, WIDE), 0)],
        [
            shape((WIDTH, WIDE), full),
            shape((RANK, WIDTH), half),
            shape((TOKENS, WIDTH), half),
        ],
        [
            pltpu.VMEM((TOKENS, WIDE), half),
            pltpu.VMEM((TOKENS, HEAD), half),
            *attention_scratch,
            *backward_scratch,
        ],
        [whole] * 3,
    )
    merged_out_0, left_0 = call(
        first_merge,
        "first_merge",
        dot_flops // 4,
        (gated_0, top, *out_parts, error_out, factor_out, left_in_0),
        [whole] * 6 + [layer_block((HEAD, WIDTH), 0), layer_block((RANK, WIDTH), 0), whole],
        [shape((HEAD, WIDTH), full), shape((RANK, WIDTH + HEAD), half)],
        [],
        [whole] * 2,
    )
    outs = compress(left_1, (merged_in_1, merged_out_1), 1, ())
    outs = compress(left_0, (merged_in_0, merged_out_0), 0, tuple(outs))
    update_in, update_out, next_in, next_out, error_in_next, error_out_next = outs
    return (
        update_in.reshape(2, 1, WIDTH, WIDE),
        update_out.reshape(2, 1, HEAD, WIDTH),
        next_in.reshape(2, 1, RANK, WIDE),
        next_out.reshape(2, 1, RANK, WIDTH),
        error_in_next.reshape(1, 2, 1, WIDTH, WIDE),
        error_out_next.reshape(1, 2, 1, HEAD, WIDTH),
    )


def solution(mesh):
    placed_in = (
        P(("rep", "tp"), None),
        P(("rep", "tp"), None),
        P(None, None, None, "tp", None),
        P(None, "tp", None, None),
        P(None, "tp", None),
        P("rep"),
        P("rep", None),
        P(None, "tp", None, None),
        P(None, "tp", None, None),
        P("rep", None, "tp", None, None),
        P("rep", None, "tp", None, None),
    )
    return jax.shard_map(
        per_device,
        mesh=mesh,
        in_specs=placed_in,
        out_specs=(
            P(None, "tp", None, None),
            P(None, "tp", None, None),
            P(None, "tp", None, None),
            P(None, "tp", None, None),
            P("rep", None, "tp", None, None),
            P("rep", None, "tp", None, None),
        ),
        check_vma=False,
    )
```

```python
import functools

import jax
import jax.numpy as jnp
from jax import lax
from jax.experimental import pallas as pl
from jax.experimental.pallas import tpu as pltpu
from jax.sharding import PartitionSpec as P

epsilon = 1e-05
highest = lax.Precision.HIGHEST
half = jnp.bfloat16
full = jnp.float32

TOKENS = 1024
WIDTH = 1024
HEAD = 128
WIDE = 4 * HEAD
RANK = 32
BUCKETS = 16
OWN = 128
BLOCK = 256
BLOCKS = TOKENS // BLOCK
MESSAGE = TOKENS + 16
SPARE_BYTES = 3 * 1024 * 1024

whole = pl.BlockSpec(memory_space=pltpu.VMEM)
scalars = pl.BlockSpec(memory_space=pltpu.SMEM)


def nn(a, b):
    return jnp.dot(a, b, preferred_element_type=full)


def nt(a, b, precision=None):
    return lax.dot_general(
        a, b, (((1,), (1,)), ((), ())), preferred_element_type=full, precision=precision
    )


def tn(a, b, precision=None):
    return lax.dot_general(
        a, b, (((0,), (0,)), ((), ())), preferred_element_type=full, precision=precision
    )


def logistic(x):
    return 0.5 * jnp.tanh(0.5 * x) + 0.5


def silu_slope(x):
    s = logistic(x)
    return s * (1.0 + x * (1.0 - s))


def centre(x):
    c = x - jnp.mean(x, axis=-1, keepdims=True)
    inverse = lax.rsqrt(jnp.mean(c * c, axis=-1, keepdims=True) + epsilon)
    return c * inverse, inverse


def split(x):
    high = x.astype(half)
    return high, (x - high.astype(full)).astype(half)


def room(dims, dtype):
    lanes = -(-dims[-1] // 128) * 128
    rows = 1
    for extent in dims[:-1]:
        rows *= extent
    return max(rows, 8) * lanes * jnp.dtype(dtype).itemsize


def call(body, name, flops, operands, in_specs, outs, scratch, out_specs=None, aliases=None):
    specs = list(in_specs) + list(out_specs or [])
    grid = {} if all(spec.block_shape is None for spec in specs) else {"grid": (1,)}
    held = 0
    for spec, array in list(zip(in_specs, operands)) + list(zip(out_specs or [whole] * len(outs), outs)):
        if spec.block_shape is not None:
            held += 2 * room(spec.block_shape, array.dtype)
        elif spec.memory_space is pltpu.VMEM:
            held += room(array.shape, array.dtype)
    moved = sum(out.size * out.dtype.itemsize for out in list(operands) + list(outs))
    return pl.pallas_call(
        body,
        name=name,
        **grid,
        out_shape=outs,
        in_specs=in_specs,
        out_specs=out_specs if out_specs is not None else [whole] * len(outs),
        scratch_shapes=scratch,
        input_output_aliases=aliases or {},
        compiler_params=pltpu.CompilerParams(
            vmem_limit_bytes=held
            + sum(room(piece.shape, piece.dtype) for piece in scratch)
            + SPARE_BYTES
        ),
        cost_estimate=pl.CostEstimate(flops=flops, bytes_accessed=moved, transcendentals=0),
    )(*operands)


def shape(dims, dtype):
    return jax.ShapeDtypeStruct(dims, dtype)


def placed(device, position):
    core = lax.rem(device, 2)
    base = device if position < 4 else device + 1 - 2 * core
    way = 2 * core - 1 if position < 4 else 1 - 2 * core
    return lax.rem(base + (0, 2 * way, -2 * way, 4)[position % 4] + 8, 8)


def rows_of(device, position):
    return pl.ds(pl.multiple_of(placed(device, position) * OWN, OWN), OWN)


def bias_operands(tables_ref, stamps_ref, hot_ref, *outs):
    scale = HEAD**-0.5
    places = lax.broadcasted_iota(jnp.int32, (HEAD, HEAD), 0)
    lanes = lax.broadcasted_iota(jnp.int32, (HEAD, HEAD), 1)
    gap = jnp.clip(places - (lanes & 63), 0, BUCKETS - 1)
    lookups = []
    for layer in range(2):
        lookup = jnp.zeros((HEAD, HEAD), full)
        for bucket in range(BUCKETS):
            lookup = jnp.where(gap == bucket, tables_ref[layer, bucket] * (1.0 / scale), lookup)
        high = lookup.astype(half).astype(full)
        lookup = jnp.where(lanes < 64, high, lookup - high)
        lookups.append(jnp.where(places < 64, lookup, 0.0).astype(half))
    first = stamps_ref[0:1, :]
    for part in range(BLOCKS):
        rows = slice(part * BLOCK, (part + 1) * BLOCK)
        since = stamps_ref[rows, :] - first
        columns = lax.broadcasted_iota(jnp.int32, (BLOCK, HEAD), 1)
        hot = jnp.where(since == (columns & 63), 1.0, 0.0)
        hot_ref[rows, :] = hot.astype(half)
        left_hot = jnp.where(columns < 64, hot, 0.0).astype(half)
        for lookup, out_ref in zip(lookups, outs):
            out_ref[rows, :] = nn(left_hot, lookup).astype(half)


def half_scores(qa_ref, ka_ref, i, j):
    return nt(
        qa_ref[i * BLOCK : (i + 1) * BLOCK, :], ka_ref[j * BLOCK : (j + 1) * BLOCK, :]
    ) * (0.5 * HEAD**-0.5)


def weights_of(qa_ref, ka_ref, i, j, with_slope):
    s = half_scores(qa_ref, ka_ref, i, j)
    double = 1.0 + jnp.tanh(s)
    w = s * double
    slope = double + w * (2.0 - double) if with_slope else None
    if i == j:
        inside = causal()
        w = jnp.where(inside, w, 0.0)
        slope = jnp.where(inside, slope, 0.0) if with_slope else None
    return w.astype(half), slope


def causal():
    return lax.broadcasted_iota(jnp.int32, (BLOCK, BLOCK), 0) >= lax.broadcasted_iota(
        jnp.int32, (BLOCK, BLOCK), 1
    )


def row_mask(i, length):
    places = lax.broadcasted_iota(jnp.int32, (BLOCK, HEAD), 0) + i * BLOCK
    return places < length


def attended_rows(total, i, length):
    return jnp.where(row_mask(i, length), total * (1.0 / length.astype(full)), 0.0)


def attend_forward(length, qa_ref, ka_ref, act_ref, gated_ref):
    for i in range(BLOCKS):
        rows = slice(i * BLOCK, (i + 1) * BLOCK)
        total = jnp.zeros((BLOCK, HEAD), full)
        for j in range(i + 1):
            w, _ = weights_of(qa_ref, ka_ref, i, j, False)
            total += nn(w, act_ref[j * BLOCK : (j + 1) * BLOCK, HEAD : 2 * HEAD])
        normed, _ = centre(attended_rows(total, i, length))
        gated_ref[rows, :] = (normed * act_ref[rows, :HEAD].astype(full)).astype(half)


def backward_rows(
    i, length, upstream, normed, inverse, weights_ref, slope_ref, act_ref, proj_slope, grad_ref, dk_ref, dv_ref
):
    rows = slice(i * BLOCK, (i + 1) * BLOCK)
    grad_ref[rows, :HEAD] = (upstream * normed * proj_slope(rows, 0)).astype(half)
    g = upstream * act_ref[rows, :HEAD].astype(full)
    back = inverse * (
        g
        - jnp.mean(g, axis=-1, keepdims=True)
        - normed * jnp.mean(g * normed, axis=-1, keepdims=True)
    )
    back = jnp.where(row_mask(i, length), back, 0.0).astype(half)
    dq = jnp.zeros((BLOCK, HEAD), full)
    for j in range(i + 1):
        cols = slice(j * BLOCK, (j + 1) * BLOCK)
        ds = (nt(back, act_ref[cols, HEAD : 2 * HEAD]) * slope_ref[:, cols].astype(full)).astype(half)
        dq += nn(ds, act_ref[cols, 3 * HEAD :])
        dk = tn(ds, act_ref[rows, 2 * HEAD : 3 * HEAD])
        dv = tn(weights_ref[:, cols], back)
        if i == j:
            dk_ref[cols, :] = dk
            dv_ref[cols, :] = dv
        else:
            dk_ref[cols, :] += dk
            dv_ref[cols, :] += dv
    factor = 0.5 * HEAD**-0.5 / length.astype(full)
    grad_ref[rows, 2 * HEAD : 3 * HEAD] = (dq * factor * proj_slope(rows, 2)).astype(half)


def backward_columns(length, proj_slope, grad_ref, dk_ref, dv_ref):
    share = 1.0 / length.astype(full)
    factor = 0.5 * HEAD**-0.5 * share
    for i in range(BLOCKS):
        rows = slice(i * BLOCK, (i + 1) * BLOCK)
        grad_ref[rows, HEAD : 2 * HEAD] = (dv_ref[rows, :] * share * proj_slope(rows, 1)).astype(half)
        grad_ref[rows, 3 * HEAD :] = (dk_ref[rows, :] * factor * proj_slope(rows, 3)).astype(half)


def activate(proj_ref, act_ref, hot_ref, bias_ref, qa_ref, ka_ref):
    for part in range(BLOCKS):
        rows = slice(part * BLOCK, (part + 1) * BLOCK)
        x = proj_ref[rows, :]
        act_ref[rows, :] = (x * logistic(x)).astype(half)
        qa_ref[rows, :HEAD] = act_ref[rows, 2 * HEAD : 3 * HEAD]
        ka_ref[rows, :HEAD] = act_ref[rows, 3 * HEAD :]
        qa_ref[rows, HEAD:] = bias_ref[rows, :]
        ka_ref[rows, HEAD:] = hot_ref[rows, :]


def first_forward(device_ref, length_ref, hot_ref, bias_ref, *refs):
    blocks = refs[:8]
    weight_ref, rows_ref, normed_ref, proj_ref, act_ref, gated_ref, qa_ref, ka_ref = refs[8:]
    device = device_ref[0]
    for position, block in enumerate(blocks):
        rows_ref[rows_of(device, position), :] = block[...]
    for part in range(BLOCKS):
        rows = slice(part * BLOCK, (part + 1) * BLOCK)
        normed = centre(rows_ref[rows, :].astype(full))[0].astype(half)
        normed_ref[rows, :] = normed
        proj_ref[rows, :] = nn(normed, weight_ref[...])
    activate(proj_ref, act_ref, hot_ref, bias_ref, qa_ref, ka_ref)
    attend_forward(length_ref[0], qa_ref, ka_ref, act_ref, gated_ref)


def attend_again(length, qa_ref, ka_ref, act_ref, weights_ref, slope_ref, attended_ref, inverse_ref, gated_ref):
    for i in range(BLOCKS):
        rows = slice(i * BLOCK, (i + 1) * BLOCK)
        total = jnp.zeros((BLOCK, HEAD), full)
        for j in range(i + 1):
            cols = slice(j * BLOCK, (j + 1) * BLOCK)
            w, slope = weights_of(qa_ref, ka_ref, i, j, True)
            weights_ref[rows, cols] = w
            slope_ref[rows, cols] = slope.astype(half)
            total += nn(w, act_ref[cols, HEAD : 2 * HEAD])
        normed, inverse = centre(attended_rows(total, i, length))
        attended_ref[rows, :] = normed
        inverse_ref[rows, :] = jnp.broadcast_to(inverse, (BLOCK, HEAD))
        if gated_ref is not None:
            gated_ref[rows, :] = (normed * act_ref[rows, :HEAD].astype(full)).astype(half)


def first_again(length_ref, hot_ref, bias_ref, proj_ref, act_ref, *refs):
    weights_ref, slope_ref, proj_slope_ref, attended_ref, inverse_ref, qa_ref, ka_ref = refs
    for part in range(BLOCKS):
        rows = slice(part * BLOCK, (part + 1) * BLOCK)
        proj_slope_ref[rows, :] = silu_slope(proj_ref[rows, :]).astype(half)
        qa_ref[rows, :HEAD] = act_ref[rows, 2 * HEAD : 3 * HEAD]
        ka_ref[rows, :HEAD] = act_ref[rows, 3 * HEAD :]
        qa_ref[rows, HEAD:] = bias_ref[rows, :]
        ka_ref[rows, HEAD:] = hot_ref[rows, :]
    attend_again(
        length_ref[0], qa_ref, ka_ref, act_ref, weights_ref, slope_ref, attended_ref, inverse_ref, None
    )


def products(*refs):
    blocks = refs[:8]
    weight_ref, mix_ref, product_ref = refs[8:]
    for position, block in enumerate(blocks):
        mix_ref[position * HEAD : (position + 1) * HEAD, :] = block[...]
    for part in range(BLOCKS):
        rows = slice(part * BLOCK, (part + 1) * BLOCK)
        product_ref[rows, :] = nn(mix_ref[rows, :], weight_ref[...]).astype(half)


def second_forward(length_ref, hot_ref, bias_ref, rows_ref, *refs):
    heads = refs[:8]
    mix_ref, weight_in_ref = refs[8:10]
    normed_ref, deviation_ref, proj_ref, proj_slope_ref, act_ref = refs[10:15]
    weights_ref, slope_ref, attended_ref, inverse_ref, gated_ref = refs[15:20]
    all_ref, qa_ref, ka_ref = refs[20:]
    for position, block in enumerate(heads):
        all_ref[:, position * HEAD : (position + 1) * HEAD] = block[...]
    for part in range(BLOCKS):
        rows = slice(part * BLOCK, (part + 1) * BLOCK)
        stream = rows_ref[rows, :].astype(full) + nn(all_ref[rows, :], mix_ref[...])
        normed, inverse = centre(stream)
        normed = normed.astype(half)
        normed_ref[rows, :] = normed
        deviation_ref[rows, :] = jnp.broadcast_to(inverse, (BLOCK, HEAD))
        projected = nn(normed, weight_in_ref[...])
        proj_ref[rows, :] = projected
        proj_slope_ref[rows, :] = silu_slope(projected).astype(half)
    activate(proj_ref, act_ref, hot_ref, bias_ref, qa_ref, ka_ref)
    attend_again(
        length_ref[0], qa_ref, ka_ref, act_ref, weights_ref, slope_ref, attended_ref, inverse_ref, gated_ref
    )


def second_backward(device_ref, length_ref, *refs):
    blocks = refs[:8]
    weight_in_ref, weight_out_ref, product_ref, inverse_ref, proj_ref = refs[8:13]
    proj_slope_ref, act_ref, weights_ref, slope_ref, attended_ref, deviation_ref = refs[13:19]
    cot_ref, grad_ref, scaled_ref, send_ref, keep_ref, dk_ref, dv_ref, sums_ref = refs[19:]
    device = device_ref[0]
    length = length_ref[0]
    for position, block in enumerate(blocks):
        cot_ref[rows_of(device, position), :] = block[...]

    def proj_slope(rows, piece):
        return proj_slope_ref[rows, piece * HEAD : (piece + 1) * HEAD].astype(full)

    for i in range(BLOCKS):
        rows = slice(i * BLOCK, (i + 1) * BLOCK)
        backward_rows(
            i,
            length,
            nt(cot_ref[rows, :], weight_out_ref[...]),
            attended_ref[rows, :],
            deviation_ref[rows, :],
            weights_ref.at[rows, :],
            slope_ref.at[rows, :],
            act_ref,
            proj_slope,
            grad_ref,
            dk_ref,
            dv_ref,
        )
    backward_columns(length, proj_slope, grad_ref, dk_ref, dv_ref)
    ones = jnp.ones((16, WIDTH), half)
    column_sum = nn(ones, weight_in_ref[...])
    high = column_sum.astype(half).astype(full)
    places = lax.broadcasted_iota(jnp.int32, (16, WIDE), 0)
    column_sum = jnp.where(
        places == 0, high, jnp.where(places == 1, column_sum - high, 0.0)
    ).astype(half)
    for part in range(BLOCKS):
        rows = slice(part * BLOCK, (part + 1) * BLOCK)
        for piece in range(4):
            lanes = slice(piece * HEAD, (piece + 1) * HEAD)
            scaled_ref[rows, lanes] = (
                grad_ref[rows, lanes].astype(full) * inverse_ref[rows, :]
            ).astype(half)
        scaled = scaled_ref[rows, :]
        by_head = nt(scaled, product_ref[...]).astype(half)
        for position in range(4):
            out = slice(position * MESSAGE + part * BLOCK, position * MESSAGE + (part + 1) * BLOCK)
            keep_ref[out, :] = by_head[:, position * HEAD : (position + 1) * HEAD]
            send_ref[out, :] = by_head[:, (position + 4) * HEAD : (position + 5) * HEAD]
        sums = nt(column_sum, scaled)
        first = sums[0:1, :] + sums[1:2, :]
        high, low = split(scaled.astype(full) * proj_ref[rows, :])
        second = (nt(ones[:, :WIDE], high) + nt(ones[:, :WIDE], low))[0:1, :]
        for piece in range(BLOCK // HEAD):
            lanes = slice(piece * HEAD, (piece + 1) * HEAD)
            row = part * (BLOCK // HEAD) + piece
            sums_ref[row : row + 1, :] = first[:, lanes]
            sums_ref[8 + row : 9 + row, :] = second[:, lanes]
    sums = sums_ref[...].astype(half)
    for position in range(4):
        out = slice(position * MESSAGE + TOKENS, (position + 1) * MESSAGE)
        keep_ref[out, :] = sums
        send_ref[out, :] = sums


def out_partials(*refs):
    heads = refs[:8]
    scaled_ref, weight_ref, send_ref, keep_ref = refs[8:]
    for position, block in enumerate(heads):
        inner = tn(block[...], scaled_ref[...]).astype(half)
        out_ref = keep_ref if position < 4 else send_ref
        out = slice(position % 4 * HEAD, (position % 4 + 1) * HEAD)
        out_ref[out, :] = nt(inner, weight_ref[...]).astype(half)


def pair_sum(keep_ref, come_ref, *outs):
    extent = keep_ref.shape[0] // 4
    for position, out in enumerate(outs):
        rows = slice(position * extent, (position + 1) * extent)
        out[...] = (keep_ref[rows, :].astype(full) + come_ref[rows, :].astype(full)).astype(half)


def left_product(factor, merged):
    high, low = split(merged)
    factor_high, factor_low = split(factor)
    both = nt(jnp.concatenate([factor_high, factor_low], axis=0), high)
    return both[:RANK] + both[RANK:] + nt(factor_high, low)


def second_merge(
    normed_ref,
    grad_ref,
    gated_ref,
    cot_ref,
    error_in_ref,
    error_out_ref,
    factor_in_ref,
    factor_out_ref,
    merged_in_ref,
    merged_out_ref,
    left_ref,
):
    merged_in = tn(normed_ref[...], grad_ref[...]).astype(half).astype(full) + error_in_ref[0]
    merged_in_ref[...] = merged_in
    left_ref[:, :WIDTH] = left_product(factor_in_ref[0], merged_in).astype(half)
    merged_out = tn(gated_ref[...], cot_ref[...]).astype(half).astype(full) + error_out_ref[0]
    merged_out_ref[...] = merged_out
    left_ref[:, WIDTH:] = left_product(factor_out_ref[0], merged_out).astype(half)


def first_sides(normed_ref, cot_ref, gated_ref, weight_ref, below_ref, upstream_ref, out_ref, sums_ref):
    below_ref[...] = nt(normed_ref[...], weight_ref[...])
    upstream_ref[...] = nt(cot_ref[...], weight_ref[...])
    out_ref[...] = tn(gated_ref[...], cot_ref[...])
    sums_ref[...] = nt(jnp.ones((16, WIDTH), half), weight_ref[...])


def spread_sums(parts, part):
    sums = four_sum(*parts, slice(TOKENS, MESSAGE), slice(None)) * (1.0 / WIDTH)
    high = sums.astype(half).astype(full)
    ones = jnp.ones((16, HEAD), half)
    places = lax.broadcasted_iota(jnp.int32, (16, HEAD), 0)
    both = []
    for row in (part, 8 + part):
        pair = jnp.where(
            places == 0,
            high[row : row + 1, :],
            jnp.where(places == 1, (sums - high)[row : row + 1, :], 0.0),
        )
        both.append(tn(pair.astype(half), ones))
    return both


def first_backward(length_ref, *refs):
    parts = refs[:4]
    weights_ref, slope_ref, proj_slope_ref, normed_ref, inverse_ref = refs[4:9]
    upstream_ref, row_sums_ref, below_ref, act_ref, above_ref = refs[9:14]
    error_in_ref, factor_in_ref = refs[14:16]
    merged_in_ref, left_ref = refs[16:18]
    grad_ref, dk_ref, dv_ref = refs[18:]
    length = length_ref[0]

    def proj_slope(rows, piece):
        return proj_slope_ref[rows, piece * HEAD : (piece + 1) * HEAD].astype(full)

    for i in range(BLOCKS):
        rows = slice(i * BLOCK, (i + 1) * BLOCK)
        taken = []
        for part in range(i * BLOCK // OWN, (i + 1) * BLOCK // OWN):
            first, second = spread_sums(parts, part)
            events = slice(part * OWN, (part + 1) * OWN)
            taken.append(first * row_sums_ref[0:1, :] + second * below_ref[events, :])
        upstream = (
            upstream_ref[rows, :]
            - jnp.concatenate(taken, axis=0)
            + four_sum(*parts, rows, slice(None))
        )
        backward_rows(
            i,
            length,
            upstream,
            normed_ref[rows, :],
            inverse_ref[rows, :],
            weights_ref.at[rows, :],
            slope_ref.at[rows, :],
            act_ref,
            proj_slope,
            grad_ref,
            dk_ref,
            dv_ref,
        )
    backward_columns(length, proj_slope, grad_ref, dk_ref, dv_ref)
    merged_in = tn(above_ref[...], grad_ref[...]).astype(half).astype(full) + error_in_ref[0]
    merged_in_ref[...] = merged_in
    left_ref[...] = left_product(factor_in_ref[0], merged_in).astype(half)


def first_merge(gated_ref, out_ref, above_ref, *refs):
    parts = refs[:4]
    heads = refs[4:8]
    error_ref, factor_ref, left_in_ref, merged_ref, left_ref, scaled_ref = refs[8:]
    firsts = jnp.zeros((HEAD, HEAD), full)
    for part in range(TOKENS // OWN):
        rows = slice(part * OWN, (part + 1) * OWN)
        first, second = spread_sums(parts, part)
        gated = gated_ref[rows, :]
        firsts += tn(gated, first.astype(half))
        scaled_ref[rows, :] = (gated.astype(full) * second).astype(half)
    everything = slice(None)
    grad = (
        out_ref[...]
        - jnp.concatenate([firsts] * (WIDTH // HEAD), axis=1)
        - tn(scaled_ref[...], above_ref[...])
        + four_sum(*heads, everything, everything)
    )
    merged = grad.astype(half).astype(full) + error_ref[0]
    merged_ref[...] = merged
    left_ref[:, :WIDTH] = left_in_ref[...]
    left_ref[:, WIDTH:] = left_product(factor_ref[0], merged).astype(half)


def four_sum(a_ref, b_ref, c_ref, d_ref, rows, columns):
    return (a_ref[rows, columns].astype(full) + c_ref[rows, columns].astype(full)) + (
        b_ref[rows, columns].astype(full) + d_ref[rows, columns].astype(full)
    )


def ring_sum(a_ref, b_ref, c_ref, d_ref, out_ref):
    everything = slice(None)
    out_ref[...] = four_sum(a_ref, b_ref, c_ref, d_ref, everything, everything).astype(half)


def cholesky_inverses(grams):
    shape_ = (RANK, 2 * RANK)
    places = lax.broadcasted_iota(jnp.int32, shape_, 0)
    unit = jnp.where(
        lax.broadcasted_iota(jnp.int32, (RANK, RANK), 0)
        == lax.broadcasted_iota(jnp.int32, (RANK, RANK), 1),
        1.0,
        0.0,
    )
    work = [jnp.concatenate([gram, unit], axis=1) for gram in grams]
    for k in range(RANK):
        for m in range(len(work)):
            a = work[m]
            root = lax.rsqrt(a[k : k + 1, k : k + 1])
            row = a[k : k + 1, :] * root
            column = jnp.where(places > k, a[:, k : k + 1] * root, 0.0)
            work[m] = jnp.where(places == k, row, a - column * row)
    return [a[:, RANK:] for a in work]


def basis_right(*refs):
    sums = refs[:4]
    merged_refs = refs[4:6]
    basis_ref, right_ref = refs[6:]
    columns = (slice(0, WIDTH), slice(WIDTH, WIDTH + HEAD))
    places = (slice(0, WIDE), slice(WIDE, WIDE + WIDTH))
    lefts = [four_sum(*sums, slice(None), column) for column in columns]
    inverses = cholesky_inverses([nt(left, left, highest) for left in lefts])
    for out in range(2):
        basis = jnp.dot(inverses[out], lefts[out], preferred_element_type=full, precision=highest)
        basis_ref[:, columns[out]] = basis
        high, low = split(merged_refs[out][...])
        basis_high, basis_low = split(basis)
        both = nn(jnp.concatenate([basis_high, basis_low], axis=0), high)
        right = both[:RANK] + both[RANK:] + nn(basis_high, low)
        right_ref[:, places[out]] = right.astype(half)


def finish(*refs):
    sums = refs[:4]
    basis_ref = refs[4]
    merged_refs = refs[5:7]
    update_in, update_out, next_in, next_out, error_in, error_out = refs[-6:]
    columns = (slice(0, WIDTH), slice(WIDTH, WIDTH + HEAD))
    places = (slice(0, WIDE), slice(WIDE, WIDE + WIDTH))
    for out in range(2):
        update_ref, next_ref, error_ref = (
            (update_out, next_out, error_out) if out else (update_in, next_in, error_in)
        )
        basis_high, basis_low = split(basis_ref[:, columns[out]])
        right = four_sum(*sums, slice(None), places[out]) * (1.0 / 16)
        next_ref[0] = right
        right_high, right_low = split(right)
        update = tn(
            jnp.concatenate([basis_high, basis_high, basis_low], axis=0),
            jnp.concatenate([right_high, right_low, right_high], axis=0),
        )
        update_ref[0] = update
        error_ref[0] = merged_refs[out][...] - update


def swap(x):
    return lax.ppermute(x, "tp", [(k, k ^ 1) for k in range(8)])


def first_way(x):
    return lax.ppermute(x, "tp", [(k, (k + 2 - 4 * (k % 2)) % 8) for k in range(8)])


def other_way(x):
    return lax.ppermute(x, "tp", [(k, (k - 2 + 4 * (k % 2)) % 8) for k in range(8)])


def across(x):
    return lax.ppermute(x, "tp", [(k, (k + 4) % 8) for k in range(8)])


def after(x, *others):
    return lax.optimization_barrier((x, *others))[0]


def gather_tp(x):
    near = first_way(x)
    mine = [x, near, other_way(x), first_way(near)]
    return mine + [swap(block) for block in mine]


def scatter_tp(send, keep, name):
    extent = (keep.shape[0] // 4, keep.shape[1])
    sums = call(
        pair_sum,
        name,
        keep.size,
        (keep, swap(send)),
        [whole] * 2,
        [shape(extent, half)] * 4,
        [],
    )
    return [sums[0], other_way(sums[1]), across(sums[3]), first_way(sums[2])], sums[1]


def ring_z(x):
    return [x] + [
        lax.ppermute(x, "rep", [(k, k - k % 4 + (k - step) % 4) for k in range(16)])
        for step in (1, 2, 3)
    ]


def ring_x(x):
    return [x] + [
        lax.ppermute(x, "rep", [(k, (k - 4 * step) % 16) for k in range(16)]) for step in (1, 2, 3)
    ]


def sum_z(x, name):
    return call(ring_sum, name, x.size * 4, ring_z(x), [whole] * 4, [shape(x.shape, half)], [])[0]


def compress(left_parts, merged, layer, others):
    basis, right = call(
        basis_right,
        f"basis_right_{layer}",
        TOKENS * WIDTH * WIDE // 4,
        (*left_parts, *merged),
        [whole] * 6,
        [shape((RANK, WIDTH + HEAD), full), shape((RANK, WIDE + WIDTH), half)],
        [],
    )
    blocks = [(WIDTH, WIDE), (HEAD, WIDTH), (RANK, WIDE), (RANK, WIDTH), (WIDTH, WIDE), (HEAD, WIDTH)]
    return call(
        finish,
        f"finish_{layer}",
        TOKENS * WIDTH * WIDE // 4,
        (*ring_x(sum_z(right, f"right_sum_{layer}")), basis, *merged, *others),
        [whole] * 7 + [pl.BlockSpec(memory_space=pl.ANY)] * len(others),
        [shape((2,) + block, full) for block in blocks],
        [],
        [layer_block(block, layer) for block in blocks],
        {7 + position: position for position in range(len(others))},
    )


def layer_block(dims, layer):
    return pl.BlockSpec((1,) + dims, lambda step: (layer, 0, 0))


def per_device(
    inputs,
    cotangent,
    weight_in,
    weight_out,
    bias_table,
    lengths,
    stamps,
    factor_in,
    factor_out,
    error_in,
    error_out,
):
    device = lax.axis_index("tp").astype(jnp.int32).reshape(1)
    stamps = stamps.reshape(TOKENS, 1)
    weight_in = weight_in.reshape(2, WIDTH, WIDE)
    weight_out = weight_out.reshape(2, HEAD, WIDTH)
    factor_in = factor_in.reshape(2, RANK, WIDE)
    factor_out = factor_out.reshape(2, RANK, WIDTH)
    error_in = error_in.reshape(2, WIDTH, WIDE)
    error_out = error_out.reshape(2, HEAD, WIDTH)

    attention_scratch = [
        pltpu.VMEM((TOKENS, 2 * HEAD), half),
        pltpu.VMEM((TOKENS, 2 * HEAD), half),
    ]
    dot_flops = 2 * TOKENS * WIDTH * WIDE
    narrow = shape((TOKENS, HEAD), half)
    narrow_full = shape((TOKENS, HEAD), full)
    square = shape((TOKENS, WIDTH), half)

    input_blocks = gather_tp(inputs)
    hot, bias_0, bias_1 = call(
        bias_operands,
        "bias_operands",
        dot_flops // 16,
        (bias_table.reshape(2, BUCKETS), stamps),
        [scalars, whole],
        [narrow] * 3,
        [],
    )
    mix = after(weight_out[0], input_blocks[3], hot)
    mix_near, mix_other = first_way(mix), other_way(mix)
    rows_all, normed_0, proj_0, act_0, gated_0 = call(
        first_forward,
        "first_forward",
        3 * dot_flops,
        (device, lengths, hot, bias_0, *input_blocks, weight_in[0]),
        [scalars] * 2 + [whole] * 11,
        [square, square, shape((TOKENS, WIDE), full), shape((TOKENS, WIDE), half), narrow],
        attention_scratch,
    )
    gated_blocks = gather_tp(gated_0)
    weights_0, slope_0, proj_slope_0, attended_0, inverse_0 = call(
        first_again,
        "first_again",
        2 * dot_flops,
        (lengths, hot, bias_0, proj_0, act_0),
        [scalars] + [whole] * 4,
        [square, square, shape((TOKENS, WIDE), half), narrow_full, narrow_full],
        attention_scratch,
    )
    mix_near = after(mix_near, weights_0)
    mix_blocks = [mix, mix_near, mix_other, first_way(mix_near)]
    mix_blocks += [swap(block) for block in mix_blocks]
    cot = after(cotangent, mix_blocks[3])
    cot_blocks = [cot, first_way(cot), other_way(cot), across(cot)]
    mix_all, product = call(
        products,
        "products",
        dot_flops,
        (*mix_blocks, weight_in[1]),
        [whole] * 9,
        [square, shape((WIDTH, WIDE), half)],
        [],
    )
    wide_full = shape((TOKENS, WIDE), full)
    wide_half = shape((TOKENS, WIDE), half)
    (
        normed_1,
        deviation_1,
        proj_1,
        proj_slope_1,
        act_1,
        weights_1,
        slope_1,
        attended_1,
        inverse_1,
        gated_1,
    ) = call(
        second_forward,
        "second_forward",
        6 * dot_flops,
        (lengths, hot, bias_1, rows_all, *gated_blocks, mix_all, weight_in[1]),
        [scalars] + [whole] * 13,
        [
            square,
            narrow_full,
            wide_full,
            wide_half,
            wide_half,
            square,
            square,
            narrow_full,
            narrow_full,
            narrow,
        ],
        [pltpu.VMEM((TOKENS, WIDTH), half), *attention_scratch],
    )
    cot_blocks += [swap(after(block, gated_1)) for block in cot_blocks]
    message = shape((4 * MESSAGE, HEAD), half)
    cot_all, grad_1, scaled_1, send, keep = call(
        second_backward,
        "second_backward",
        6 * dot_flops,
        (
            device,
            lengths,
            *cot_blocks,
            weight_in[1],
            weight_out[1],
            product,
            deviation_1,
            proj_1,
            proj_slope_1,
            act_1,
            weights_1,
            slope_1,
            attended_1,
            inverse_1,
        ),
        [scalars] * 2 + [whole] * 19,
        [square, wide_half, wide_half, message, message],
        [
            pltpu.VMEM((TOKENS, HEAD), full),
            pltpu.VMEM((TOKENS, HEAD), full),
            pltpu.VMEM((16, HEAD), full),
        ],
    )
    gated_parts, gated_sums = scatter_tp(send, keep, "gated_pairs")
    out_send, out_keep = call(
        out_partials,
        "out_partials",
        2 * dot_flops,
        (*gated_blocks, scaled_1, weight_in[1]),
        [whole] * 10,
        [shape((4 * HEAD, WIDTH), half)] * 2,
        [],
    )
    out_parts, _ = scatter_tp(out_send, out_keep, "out_pairs")
    merged_shapes = [shape((WIDTH, WIDE), full), shape((HEAD, WIDTH), full)]
    merged_in_1, merged_out_1, left_1 = call(
        second_merge,
        "second_merge",
        3 * dot_flops,
        (
            after(normed_1, gated_sums),
            grad_1,
            gated_1,
            cot_all,
            error_in,
            error_out,
            factor_in,
            factor_out,
        ),
        [whole] * 4
        + [
            layer_block((WIDTH, WIDE), 1),
            layer_block((HEAD, WIDTH), 1),
            layer_block((RANK, WIDE), 1),
            layer_block((RANK, WIDTH), 1),
        ],
        merged_shapes + [shape((RANK, WIDTH + HEAD), half)],
        [],
        [whole] * 3,
    )
    below_0, upstream_0, out_0, row_sums = call(
        first_sides,
        "first_sides",
        dot_flops,
        (normed_1, after(cot_all, gated_sums), gated_0, weight_out[0]),
        [whole] * 4,
        [narrow_full, narrow_full, shape((HEAD, WIDTH), full), shape((16, HEAD), full)],
        [],
    )

    left_1 = sum_z(left_1, "left_sum_1")
    merged_in_0, left_in_0 = call(
        first_backward,
        "first_backward",
        6 * dot_flops,
        (
            lengths,
            *gated_parts,
            weights_0,
            slope_0,
            proj_slope_0,
            attended_0,
            inverse_0,
            upstream_0,
            row_sums,
            after(below_0, left_1),
            act_0,
            normed_0,
            error_in,
            factor_in,
        ),
        [scalars] + [whole] * 14 + [layer_block((WIDTH, WIDE), 0), layer_block((RANK, WIDE), 0)],
        [shape((WIDTH, WIDE), full), shape((RANK, WIDTH), half)],
        [
            pltpu.VMEM((TOKENS, WIDE), half),
            pltpu.VMEM((TOKENS, HEAD), full),
            pltpu.VMEM((TOKENS, HEAD), full),
        ],
        [whole] * 2,
    )
    left_parts_1 = ring_x(left_1)
    merged_out_0, left_0 = call(
        first_merge,
        "first_merge",
        dot_flops // 4,
        (gated_0, out_0, normed_1, *gated_parts, *out_parts, error_out, factor_out, after(left_in_0, left_parts_1[1])),
        [whole] * 11 + [layer_block((HEAD, WIDTH), 0), layer_block((RANK, WIDTH), 0), whole],
        [shape((HEAD, WIDTH), full), shape((RANK, WIDTH + HEAD), half)],
        [pltpu.VMEM((TOKENS, HEAD), half)],
        [whole] * 2,
    )
    left_0 = sum_z(left_0, "left_sum_0")
    outs = compress(left_parts_1, (merged_in_1, merged_out_1), 1, ())
    outs = compress(ring_x(left_0), (merged_in_0, merged_out_0), 0, tuple(outs))
    update_in, update_out, next_in, next_out, error_in_next, error_out_next = outs
    return (
        update_in.reshape(2, 1, WIDTH, WIDE),
        update_out.reshape(2, 1, HEAD, WIDTH),
        next_in.reshape(2, 1, RANK, WIDE),
        next_out.reshape(2, 1, RANK, WIDTH),
        error_in_next.reshape(1, 2, 1, WIDTH, WIDE),
        error_out_next.reshape(1, 2, 1, HEAD, WIDTH),
    )


def solution(mesh):
    placed_in = (
        P(("rep", "tp"), None),
        P(("rep", "tp"), None),
        P(None, None, None, "tp", None),
        P(None, "tp", None, None),
        P(None, "tp", None),
        P("rep"),
        P("rep", None),
        P(None, "tp", None, None),
        P(None, "tp", None, None),
        P("rep", None, "tp", None, None),
        P("rep", None, "tp", None, None),
    )
    return jax.shard_map(
        per_device,
        mesh=mesh,
        in_specs=placed_in,
        out_specs=(
            P(None, "tp", None, None),
            P(None, "tp", None, None),
            P(None, "tp", None, None),
            P(None, "tp", None, None),
            P("rep", None, "tp", None, None),
            P("rep", None, "tp", None, None),
        ),
        check_vma=False,
    )
```

```python
import functools

import jax
import jax.numpy as jnp
from jax import lax
from jax.experimental import pallas as pl
from jax.experimental.pallas import tpu as pltpu
from jax.sharding import PartitionSpec as P

epsilon = 1e-05
highest = lax.Precision.HIGHEST
half = jnp.bfloat16
full = jnp.float32

TOKENS = 1024
WIDTH = 1024
HEAD = 128
WIDE = 4 * HEAD
RANK = 32
BUCKETS = 16
OWN = 128
BLOCK = 256
BLOCKS = TOKENS // BLOCK
MESSAGE = TOKENS + 16
SPARE_BYTES = 3 * 1024 * 1024

whole = pl.BlockSpec(memory_space=pltpu.VMEM)
scalars = pl.BlockSpec(memory_space=pltpu.SMEM)


def nn(a, b):
    return jnp.dot(a, b, preferred_element_type=full)


def nt(a, b, precision=None):
    return lax.dot_general(
        a, b, (((1,), (1,)), ((), ())), preferred_element_type=full, precision=precision
    )


def tn(a, b, precision=None):
    return lax.dot_general(
        a, b, (((0,), (0,)), ((), ())), preferred_element_type=full, precision=precision
    )


def logistic(x):
    return 0.5 * jnp.tanh(0.5 * x) + 0.5


def silu_slope(x):
    s = logistic(x)
    return s * (1.0 + x * (1.0 - s))


def centre(x):
    c = x - jnp.mean(x, axis=-1, keepdims=True)
    inverse = lax.rsqrt(jnp.mean(c * c, axis=-1, keepdims=True) + epsilon)
    return c * inverse, inverse


def split(x):
    high = x.astype(half)
    return high, (x - high.astype(full)).astype(half)


def room(dims, dtype):
    lanes = -(-dims[-1] // 128) * 128
    rows = 1
    for extent in dims[:-1]:
        rows *= extent
    return max(rows, 8) * lanes * jnp.dtype(dtype).itemsize


def call(body, name, flops, operands, in_specs, outs, scratch, out_specs=None, aliases=None):
    specs = list(in_specs) + list(out_specs or [])
    grid = {} if all(spec.block_shape is None for spec in specs) else {"grid": (1,)}
    held = 0
    for spec, array in list(zip(in_specs, operands)) + list(zip(out_specs or [whole] * len(outs), outs)):
        if spec.block_shape is not None:
            held += 2 * room(spec.block_shape, array.dtype)
        elif spec.memory_space is pltpu.VMEM:
            held += room(array.shape, array.dtype)
    moved = sum(out.size * out.dtype.itemsize for out in list(operands) + list(outs))
    return pl.pallas_call(
        body,
        name=name,
        **grid,
        out_shape=outs,
        in_specs=in_specs,
        out_specs=out_specs if out_specs is not None else [whole] * len(outs),
        scratch_shapes=scratch,
        input_output_aliases=aliases or {},
        compiler_params=pltpu.CompilerParams(
            vmem_limit_bytes=held
            + sum(room(piece.shape, piece.dtype) for piece in scratch)
            + SPARE_BYTES
        ),
        cost_estimate=pl.CostEstimate(flops=flops, bytes_accessed=moved, transcendentals=0),
    )(*operands)


def shape(dims, dtype):
    return jax.ShapeDtypeStruct(dims, dtype)


def placed(device, position):
    core = lax.rem(device, 2)
    base = device if position < 4 else device + 1 - 2 * core
    way = 2 * core - 1 if position < 4 else 1 - 2 * core
    return lax.rem(base + (0, 2 * way, -2 * way, 4)[position % 4] + 8, 8)


def rows_of(device, position):
    return pl.ds(pl.multiple_of(placed(device, position) * OWN, OWN), OWN)


def bias_operands(tables_ref, stamps_ref, hot_ref, *outs):
    scale = HEAD**-0.5
    places = lax.broadcasted_iota(jnp.int32, (HEAD, HEAD), 0)
    lanes = lax.broadcasted_iota(jnp.int32, (HEAD, HEAD), 1)
    gap = jnp.clip(places - (lanes & 63), 0, BUCKETS - 1)
    lookups = []
    for layer in range(2):
        lookup = jnp.zeros((HEAD, HEAD), full)
        for bucket in range(BUCKETS):
            lookup = jnp.where(gap == bucket, tables_ref[layer, bucket] * (1.0 / scale), lookup)
        high = lookup.astype(half).astype(full)
        lookup = jnp.where(lanes < 64, high, lookup - high)
        lookups.append(jnp.where(places < 64, lookup, 0.0).astype(half))
    first = stamps_ref[0:1, :]
    for part in range(BLOCKS):
        rows = slice(part * BLOCK, (part + 1) * BLOCK)
        since = stamps_ref[rows, :] - first
        columns = lax.broadcasted_iota(jnp.int32, (BLOCK, HEAD), 1)
        hot = jnp.where(since == (columns & 63), 1.0, 0.0)
        hot_ref[rows, :] = hot.astype(half)
        left_hot = jnp.where(columns < 64, hot, 0.0).astype(half)
        for lookup, out_ref in zip(lookups, outs):
            out_ref[rows, :] = nn(left_hot, lookup).astype(half)


def half_scores(qa_ref, ka_ref, i, j):
    return nt(
        qa_ref[i * BLOCK : (i + 1) * BLOCK, :], ka_ref[j * BLOCK : (j + 1) * BLOCK, :]
    ) * (0.5 * HEAD**-0.5)


def weights_of(qa_ref, ka_ref, i, j, with_slope):
    s = half_scores(qa_ref, ka_ref, i, j)
    double = 1.0 + jnp.tanh(s)
    w = s * double
    slope = double + w * (2.0 - double) if with_slope else None
    if i == j:
        inside = causal()
        w = jnp.where(inside, w, 0.0)
        slope = jnp.where(inside, slope, 0.0) if with_slope else None
    return w.astype(half), slope


def causal():
    return lax.broadcasted_iota(jnp.int32, (BLOCK, BLOCK), 0) >= lax.broadcasted_iota(
        jnp.int32, (BLOCK, BLOCK), 1
    )


def row_mask(i, length):
    places = lax.broadcasted_iota(jnp.int32, (BLOCK, HEAD), 0) + i * BLOCK
    return places < length


def attended_rows(total, i, length):
    return jnp.where(row_mask(i, length), total * (1.0 / length.astype(full)), 0.0)


def attend_forward(length, qa_ref, ka_ref, act_ref, gated_ref):
    for i in range(BLOCKS):
        rows = slice(i * BLOCK, (i + 1) * BLOCK)
        total = jnp.zeros((BLOCK, HEAD), full)
        for j in range(i + 1):
            w, _ = weights_of(qa_ref, ka_ref, i, j, False)
            total += nn(w, act_ref[j * BLOCK : (j + 1) * BLOCK, HEAD : 2 * HEAD])
        normed, _ = centre(attended_rows(total, i, length))
        gated_ref[rows, :] = (normed * act_ref[rows, :HEAD].astype(full)).astype(half)


def backward_rows(
    i, length, upstream, normed, inverse, weights_ref, slope_ref, act_ref, proj_slope, grad_ref, dk_ref, dv_ref
):
    rows = slice(i * BLOCK, (i + 1) * BLOCK)
    grad_ref[rows, :HEAD] = (upstream * normed * proj_slope(rows, 0)).astype(half)
    g = upstream * act_ref[rows, :HEAD].astype(full)
    back = inverse * (
        g
        - jnp.mean(g, axis=-1, keepdims=True)
        - normed * jnp.mean(g * normed, axis=-1, keepdims=True)
    )
    back = jnp.where(row_mask(i, length), back, 0.0).astype(half)
    dq = jnp.zeros((BLOCK, HEAD), full)
    for j in range(i + 1):
        cols = slice(j * BLOCK, (j + 1) * BLOCK)
        ds = (nt(back, act_ref[cols, HEAD : 2 * HEAD]) * slope_ref[:, cols].astype(full)).astype(half)
        dq += nn(ds, act_ref[cols, 3 * HEAD :])
        dk = tn(ds, act_ref[rows, 2 * HEAD : 3 * HEAD])
        dv = tn(weights_ref[:, cols], back)
        if i == j:
            dk_ref[cols, :] = dk
            dv_ref[cols, :] = dv
        else:
            dk_ref[cols, :] += dk
            dv_ref[cols, :] += dv
    factor = 0.5 * HEAD**-0.5 / length.astype(full)
    grad_ref[rows, 2 * HEAD : 3 * HEAD] = (dq * factor * proj_slope(rows, 2)).astype(half)


def backward_columns(length, proj_slope, grad_ref, dk_ref, dv_ref):
    share = 1.0 / length.astype(full)
    factor = 0.5 * HEAD**-0.5 * share
    for i in range(BLOCKS):
        rows = slice(i * BLOCK, (i + 1) * BLOCK)
        grad_ref[rows, HEAD : 2 * HEAD] = (dv_ref[rows, :] * share * proj_slope(rows, 1)).astype(half)
        grad_ref[rows, 3 * HEAD :] = (dk_ref[rows, :] * factor * proj_slope(rows, 3)).astype(half)


def activate(proj_ref, act_ref, hot_ref, bias_ref, qa_ref, ka_ref):
    for part in range(BLOCKS):
        rows = slice(part * BLOCK, (part + 1) * BLOCK)
        x = proj_ref[rows, :]
        act_ref[rows, :] = (x * logistic(x)).astype(half)
        qa_ref[rows, :HEAD] = act_ref[rows, 2 * HEAD : 3 * HEAD]
        ka_ref[rows, :HEAD] = act_ref[rows, 3 * HEAD :]
        qa_ref[rows, HEAD:] = bias_ref[rows, :]
        ka_ref[rows, HEAD:] = hot_ref[rows, :]


def first_forward(device_ref, length_ref, hot_ref, bias_ref, *refs):
    blocks = refs[:8]
    weight_ref, rows_ref, normed_ref, proj_ref, act_ref, gated_ref, qa_ref, ka_ref = refs[8:]
    device = device_ref[0]
    for position, block in enumerate(blocks):
        rows_ref[rows_of(device, position), :] = block[...]
    for part in range(BLOCKS):
        rows = slice(part * BLOCK, (part + 1) * BLOCK)
        normed = centre(rows_ref[rows, :].astype(full))[0].astype(half)
        normed_ref[rows, :] = normed
        proj_ref[rows, :] = nn(normed, weight_ref[...])
    activate(proj_ref, act_ref, hot_ref, bias_ref, qa_ref, ka_ref)
    attend_forward(length_ref[0], qa_ref, ka_ref, act_ref, gated_ref)


def attend_again(length, qa_ref, ka_ref, act_ref, weights_ref, slope_ref, attended_ref, inverse_ref, gated_ref):
    for i in range(BLOCKS):
        rows = slice(i * BLOCK, (i + 1) * BLOCK)
        total = jnp.zeros((BLOCK, HEAD), full)
        for j in range(i + 1):
            cols = slice(j * BLOCK, (j + 1) * BLOCK)
            w, slope = weights_of(qa_ref, ka_ref, i, j, True)
            weights_ref[rows, cols] = w
            slope_ref[rows, cols] = slope.astype(half)
            total += nn(w, act_ref[cols, HEAD : 2 * HEAD])
        normed, inverse = centre(attended_rows(total, i, length))
        attended_ref[rows, :] = normed
        inverse_ref[rows, :] = jnp.broadcast_to(inverse, (BLOCK, HEAD))
        if gated_ref is not None:
            gated_ref[rows, :] = (normed * act_ref[rows, :HEAD].astype(full)).astype(half)


def first_again(length_ref, hot_ref, bias_ref, proj_ref, act_ref, *refs):
    weights_ref, slope_ref, proj_slope_ref, attended_ref, inverse_ref, qa_ref, ka_ref = refs
    for part in range(BLOCKS):
        rows = slice(part * BLOCK, (part + 1) * BLOCK)
        proj_slope_ref[rows, :] = silu_slope(proj_ref[rows, :]).astype(half)
        qa_ref[rows, :HEAD] = act_ref[rows, 2 * HEAD : 3 * HEAD]
        ka_ref[rows, :HEAD] = act_ref[rows, 3 * HEAD :]
        qa_ref[rows, HEAD:] = bias_ref[rows, :]
        ka_ref[rows, HEAD:] = hot_ref[rows, :]
    attend_again(
        length_ref[0], qa_ref, ka_ref, act_ref, weights_ref, slope_ref, attended_ref, inverse_ref, None
    )


def products(*refs):
    blocks = refs[:8]
    weight_ref, mix_ref, product_ref = refs[8:]
    for position, block in enumerate(blocks):
        mix_ref[position * HEAD : (position + 1) * HEAD, :] = block[...]
    for part in range(BLOCKS):
        rows = slice(part * BLOCK, (part + 1) * BLOCK)
        product_ref[rows, :] = nn(mix_ref[rows, :], weight_ref[...]).astype(half)


def second_forward(length_ref, hot_ref, bias_ref, rows_ref, *refs):
    heads = refs[:8]
    mix_ref, weight_in_ref = refs[8:10]
    normed_ref, deviation_ref, proj_ref, proj_slope_ref, act_ref = refs[10:15]
    weights_ref, slope_ref, attended_ref, inverse_ref, gated_ref = refs[15:20]
    all_ref, qa_ref, ka_ref = refs[20:]
    for position, block in enumerate(heads):
        all_ref[:, position * HEAD : (position + 1) * HEAD] = block[...]
    for part in range(BLOCKS):
        rows = slice(part * BLOCK, (part + 1) * BLOCK)
        stream = rows_ref[rows, :].astype(full) + nn(all_ref[rows, :], mix_ref[...])
        normed, inverse = centre(stream)
        normed = normed.astype(half)
        normed_ref[rows, :] = normed
        deviation_ref[rows, :] = jnp.broadcast_to(inverse, (BLOCK, HEAD))
        projected = nn(normed, weight_in_ref[...])
        proj_ref[rows, :] = projected
        proj_slope_ref[rows, :] = silu_slope(projected).astype(half)
    activate(proj_ref, act_ref, hot_ref, bias_ref, qa_ref, ka_ref)
    attend_again(
        length_ref[0], qa_ref, ka_ref, act_ref, weights_ref, slope_ref, attended_ref, inverse_ref, gated_ref
    )


def second_backward(device_ref, length_ref, *refs):
    blocks = refs[:8]
    weight_in_ref, weight_out_ref, product_ref, inverse_ref, proj_ref = refs[8:13]
    proj_slope_ref, act_ref, weights_ref, slope_ref, attended_ref, deviation_ref = refs[13:19]
    cot_ref, grad_ref, scaled_ref, send_ref, keep_ref, dk_ref, dv_ref, sums_ref = refs[19:]
    device = device_ref[0]
    length = length_ref[0]
    for position, block in enumerate(blocks):
        cot_ref[rows_of(device, position), :] = block[...]

    def proj_slope(rows, piece):
        return proj_slope_ref[rows, piece * HEAD : (piece + 1) * HEAD].astype(full)

    for i in range(BLOCKS):
        rows = slice(i * BLOCK, (i + 1) * BLOCK)
        backward_rows(
            i,
            length,
            nt(cot_ref[rows, :], weight_out_ref[...]),
            attended_ref[rows, :],
            deviation_ref[rows, :],
            weights_ref.at[rows, :],
            slope_ref.at[rows, :],
            act_ref,
            proj_slope,
            grad_ref,
            dk_ref,
            dv_ref,
        )
    backward_columns(length, proj_slope, grad_ref, dk_ref, dv_ref)
    ones = jnp.ones((16, WIDTH), half)
    column_sum = nn(ones, weight_in_ref[...])
    high = column_sum.astype(half).astype(full)
    places = lax.broadcasted_iota(jnp.int32, (16, WIDE), 0)
    column_sum = jnp.where(
        places == 0, high, jnp.where(places == 1, column_sum - high, 0.0)
    ).astype(half)
    for part in range(BLOCKS):
        rows = slice(part * BLOCK, (part + 1) * BLOCK)
        for piece in range(4):
            lanes = slice(piece * HEAD, (piece + 1) * HEAD)
            scaled_ref[rows, lanes] = (
                grad_ref[rows, lanes].astype(full) * inverse_ref[rows, :]
            ).astype(half)
        scaled = scaled_ref[rows, :]
        by_head = nt(scaled, product_ref[...]).astype(half)
        for position in range(4):
            out = slice(position * MESSAGE + part * BLOCK, position * MESSAGE + (part + 1) * BLOCK)
            keep_ref[out, :] = by_head[:, position * HEAD : (position + 1) * HEAD]
            send_ref[out, :] = by_head[:, (position + 4) * HEAD : (position + 5) * HEAD]
        sums = nt(column_sum, scaled)
        first = sums[0:1, :] + sums[1:2, :]
        high, low = split(scaled.astype(full) * proj_ref[rows, :])
        second = (nt(ones[:, :WIDE], high) + nt(ones[:, :WIDE], low))[0:1, :]
        for piece in range(BLOCK // HEAD):
            lanes = slice(piece * HEAD, (piece + 1) * HEAD)
            row = part * (BLOCK // HEAD) + piece
            sums_ref[row : row + 1, :] = first[:, lanes]
            sums_ref[8 + row : 9 + row, :] = second[:, lanes]
    sums = sums_ref[...].astype(half)
    for position in range(4):
        out = slice(position * MESSAGE + TOKENS, (position + 1) * MESSAGE)
        keep_ref[out, :] = sums
        send_ref[out, :] = sums


def out_partials(*refs):
    heads = refs[:4]
    scaled_ref, weight_ref, out_ref = refs[4:]
    for position, block in enumerate(heads):
        inner = tn(block[...], scaled_ref[...]).astype(half)
        out_ref[position * HEAD : (position + 1) * HEAD, :] = nt(inner, weight_ref[...]).astype(half)


def pair_sum(keep_ref, come_ref, *outs):
    extent = keep_ref.shape[0] // 4
    for position, out in enumerate(outs):
        rows = slice(position * extent, (position + 1) * extent)
        out[...] = (keep_ref[rows, :].astype(full) + come_ref[rows, :].astype(full)).astype(half)


def left_product(factor, merged):
    high, low = split(merged)
    factor_high, factor_low = split(factor)
    both = nt(jnp.concatenate([factor_high, factor_low], axis=0), high)
    return both[:RANK] + both[RANK:] + nt(factor_high, low)


def second_merge(
    normed_ref,
    grad_ref,
    gated_ref,
    cot_ref,
    error_in_ref,
    error_out_ref,
    factor_in_ref,
    factor_out_ref,
    merged_in_ref,
    merged_out_ref,
    left_ref,
):
    merged_in = tn(normed_ref[...], grad_ref[...]).astype(half).astype(full) + error_in_ref[0]
    merged_in_ref[...] = merged_in
    left_ref[:, :WIDTH] = left_product(factor_in_ref[0], merged_in).astype(half)
    merged_out = tn(gated_ref[...], cot_ref[...]).astype(half).astype(full) + error_out_ref[0]
    merged_out_ref[...] = merged_out
    left_ref[:, WIDTH:] = left_product(factor_out_ref[0], merged_out).astype(half)


def first_sides(normed_ref, cot_ref, gated_ref, weight_ref, below_ref, upstream_ref, out_ref, sums_ref):
    below_ref[...] = nt(normed_ref[...], weight_ref[...])
    upstream_ref[...] = nt(cot_ref[...], weight_ref[...])
    out_ref[...] = tn(gated_ref[...], cot_ref[...])
    sums_ref[...] = nt(jnp.ones((16, WIDTH), half), weight_ref[...])


def spread_sums(parts, part):
    sums = four_sum(*parts, slice(TOKENS, MESSAGE), slice(None)) * (1.0 / WIDTH)
    high = sums.astype(half).astype(full)
    ones = jnp.ones((16, HEAD), half)
    places = lax.broadcasted_iota(jnp.int32, (16, HEAD), 0)
    both = []
    for row in (part, 8 + part):
        pair = jnp.where(
            places == 0,
            high[row : row + 1, :],
            jnp.where(places == 1, (sums - high)[row : row + 1, :], 0.0),
        )
        both.append(tn(pair.astype(half), ones))
    return both


def first_backward(length_ref, *refs):
    parts = refs[:4]
    weights_ref, slope_ref, proj_slope_ref, normed_ref, inverse_ref = refs[4:9]
    upstream_ref, row_sums_ref, below_ref, act_ref, above_ref = refs[9:14]
    error_in_ref, factor_in_ref = refs[14:16]
    merged_in_ref, left_ref = refs[16:18]
    grad_ref, dk_ref, dv_ref = refs[18:]
    length = length_ref[0]

    def proj_slope(rows, piece):
        return proj_slope_ref[rows, piece * HEAD : (piece + 1) * HEAD].astype(full)

    for i in range(BLOCKS):
        rows = slice(i * BLOCK, (i + 1) * BLOCK)
        taken = []
        for part in range(i * BLOCK // OWN, (i + 1) * BLOCK // OWN):
            first, second = spread_sums(parts, part)
            events = slice(part * OWN, (part + 1) * OWN)
            taken.append(first * row_sums_ref[0:1, :] + second * below_ref[events, :])
        upstream = (
            upstream_ref[rows, :]
            - jnp.concatenate(taken, axis=0)
            + four_sum(*parts, rows, slice(None))
        )
        backward_rows(
            i,
            length,
            upstream,
            normed_ref[rows, :],
            inverse_ref[rows, :],
            weights_ref.at[rows, :],
            slope_ref.at[rows, :],
            act_ref,
            proj_slope,
            grad_ref,
            dk_ref,
            dv_ref,
        )
    backward_columns(length, proj_slope, grad_ref, dk_ref, dv_ref)
    merged_in = tn(above_ref[...], grad_ref[...]).astype(half).astype(full) + error_in_ref[0]
    merged_in_ref[...] = merged_in
    left_ref[...] = left_product(factor_in_ref[0], merged_in).astype(half)


def first_merge(gated_ref, out_ref, above_ref, *refs):
    parts = refs[:4]
    heads = refs[4:8]
    error_ref, factor_ref, left_in_ref, merged_ref, left_ref, scaled_ref = refs[8:]
    firsts = jnp.zeros((HEAD, HEAD), full)
    for part in range(TOKENS // OWN):
        rows = slice(part * OWN, (part + 1) * OWN)
        first, second = spread_sums(parts, part)
        gated = gated_ref[rows, :]
        firsts += tn(gated, first.astype(half))
        scaled_ref[rows, :] = (gated.astype(full) * second).astype(half)
    everything = slice(None)
    grad = (
        out_ref[...]
        - jnp.concatenate([firsts] * (WIDTH // HEAD), axis=1)
        - tn(scaled_ref[...], above_ref[...])
        + four_sum(*heads, everything, everything)
    )
    merged = grad.astype(half).astype(full) + error_ref[0]
    merged_ref[...] = merged
    left_ref[:, :WIDTH] = left_in_ref[...]
    left_ref[:, WIDTH:] = left_product(factor_ref[0], merged).astype(half)


def four_sum(a_ref, b_ref, c_ref, d_ref, rows, columns):
    return (a_ref[rows, columns].astype(full) + c_ref[rows, columns].astype(full)) + (
        b_ref[rows, columns].astype(full) + d_ref[rows, columns].astype(full)
    )


def ring_sum(a_ref, b_ref, c_ref, d_ref, out_ref):
    everything = slice(None)
    out_ref[...] = four_sum(a_ref, b_ref, c_ref, d_ref, everything, everything).astype(half)


def cholesky_inverses(grams):
    shape_ = (RANK, 2 * RANK)
    places = lax.broadcasted_iota(jnp.int32, shape_, 0)
    unit = jnp.where(
        lax.broadcasted_iota(jnp.int32, (RANK, RANK), 0)
        == lax.broadcasted_iota(jnp.int32, (RANK, RANK), 1),
        1.0,
        0.0,
    )
    work = [jnp.concatenate([gram, unit], axis=1) for gram in grams]
    for k in range(0, RANK, 2):
        for m in range(len(work)):
            a = work[m]
            root = lax.rsqrt(a[k : k + 1, k : k + 1])
            cross = a[k : k + 1, k + 1 : k + 2] * root
            next_root = lax.rsqrt(a[k + 1 : k + 2, k + 1 : k + 2] - cross * cross)
            row = a[k : k + 1, :] * root
            column = a[:, k : k + 1] * root
            next_row = (a[k + 1 : k + 2, :] - cross * row) * next_root
            next_column = (a[:, k + 1 : k + 2] - column * cross) * next_root
            a = jnp.where(places > k + 1, a - column * row - next_column * next_row, a)
            a = jnp.where(places == k, row, a)
            work[m] = jnp.where(places == k + 1, next_row, a)
    return [a[:, RANK:] for a in work]


def basis_right(*refs):
    sums = refs[:4]
    merged_refs = refs[4:6]
    basis_ref, right_ref = refs[6:]
    columns = (slice(0, WIDTH), slice(WIDTH, WIDTH + HEAD))
    places = (slice(0, WIDE), slice(WIDE, WIDE + WIDTH))
    lefts = [four_sum(*sums, slice(None), column) for column in columns]
    inverses = cholesky_inverses([nt(left, left, highest) for left in lefts])
    for out in range(2):
        basis = jnp.dot(inverses[out], lefts[out], preferred_element_type=full, precision=highest)
        basis_ref[:, columns[out]] = basis
        high, low = split(merged_refs[out][...])
        basis_high, basis_low = split(basis)
        both = nn(jnp.concatenate([basis_high, basis_low], axis=0), high)
        right = both[:RANK] + both[RANK:] + nn(basis_high, low)
        right_ref[:, places[out]] = right.astype(half)


def finish(*refs):
    sums = refs[:4]
    basis_ref = refs[4]
    merged_refs = refs[5:7]
    update_in, update_out, next_in, next_out, error_in, error_out = refs[-6:]
    columns = (slice(0, WIDTH), slice(WIDTH, WIDTH + HEAD))
    places = (slice(0, WIDE), slice(WIDE, WIDE + WIDTH))
    for out in range(2):
        update_ref, next_ref, error_ref = (
            (update_out, next_out, error_out) if out else (update_in, next_in, error_in)
        )
        basis_high, basis_low = split(basis_ref[:, columns[out]])
        right = four_sum(*sums, slice(None), places[out]) * (1.0 / 16)
        next_ref[0] = right
        right_high, right_low = split(right)
        update = tn(
            jnp.concatenate([basis_high, basis_high, basis_low], axis=0),
            jnp.concatenate([right_high, right_low, right_high], axis=0),
        )
        update_ref[0] = update
        error_ref[0] = merged_refs[out][...] - update


def swap(x):
    return lax.ppermute(x, "tp", [(k, k ^ 1) for k in range(8)])


def first_way(x):
    return lax.ppermute(x, "tp", [(k, (k + 2 - 4 * (k % 2)) % 8) for k in range(8)])


def other_way(x):
    return lax.ppermute(x, "tp", [(k, (k - 2 + 4 * (k % 2)) % 8) for k in range(8)])


def across(x):
    return lax.ppermute(x, "tp", [(k, (k + 4) % 8) for k in range(8)])


def after(x, *others):
    return lax.optimization_barrier((x, *others))[0]


def gather_tp(x):
    near = first_way(x)
    mine = [x, near, other_way(x), first_way(near)]
    return mine + [swap(block) for block in mine]


def scatter_tp(send, keep, name):
    extent = (keep.shape[0] // 4, keep.shape[1])
    sums = call(
        pair_sum,
        name,
        keep.size,
        (keep, swap(send)),
        [whole] * 2,
        [shape(extent, half)] * 4,
        [],
    )
    return [sums[0], other_way(sums[1]), across(sums[3]), first_way(sums[2])], sums[1]


def ring_z(x):
    return [x] + [
        lax.ppermute(x, "rep", [(k, k - k % 4 + (k - step) % 4) for k in range(16)])
        for step in (1, 2, 3)
    ]


def ring_x(x):
    return [x] + [
        lax.ppermute(x, "rep", [(k, (k - 4 * step) % 16) for k in range(16)]) for step in (1, 2, 3)
    ]


def sum_z(x, name):
    return call(ring_sum, name, x.size * 4, ring_z(x), [whole] * 4, [shape(x.shape, half)], [])[0]


def compress(left_parts, merged, layer, others):
    basis, right = call(
        basis_right,
        f"basis_right_{layer}",
        TOKENS * WIDTH * WIDE // 4,
        (*left_parts, *merged),
        [whole] * 6,
        [shape((RANK, WIDTH + HEAD), full), shape((RANK, WIDE + WIDTH), half)],
        [],
    )
    blocks = [(WIDTH, WIDE), (HEAD, WIDTH), (RANK, WIDE), (RANK, WIDTH), (WIDTH, WIDE), (HEAD, WIDTH)]
    return call(
        finish,
        f"finish_{layer}",
        TOKENS * WIDTH * WIDE // 4,
        (*ring_x(sum_z(right, f"right_sum_{layer}")), basis, *merged, *others),
        [whole] * 7 + [pl.BlockSpec(memory_space=pl.ANY)] * len(others),
        [shape((2,) + block, full) for block in blocks],
        [],
        [layer_block(block, layer) for block in blocks],
        {7 + position: position for position in range(len(others))},
    )


def layer_block(dims, layer):
    return pl.BlockSpec((1,) + dims, lambda step: (layer, 0, 0))


def per_device(
    inputs,
    cotangent,
    weight_in,
    weight_out,
    bias_table,
    lengths,
    stamps,
    factor_in,
    factor_out,
    error_in,
    error_out,
):
    device = lax.axis_index("tp").astype(jnp.int32).reshape(1)
    stamps = stamps.reshape(TOKENS, 1)
    weight_in = weight_in.reshape(2, WIDTH, WIDE)
    weight_out = weight_out.reshape(2, HEAD, WIDTH)
    factor_in = factor_in.reshape(2, RANK, WIDE)
    factor_out = factor_out.reshape(2, RANK, WIDTH)
    error_in = error_in.reshape(2, WIDTH, WIDE)
    error_out = error_out.reshape(2, HEAD, WIDTH)

    attention_scratch = [
        pltpu.VMEM((TOKENS, 2 * HEAD), half),
        pltpu.VMEM((TOKENS, 2 * HEAD), half),
    ]
    dot_flops = 2 * TOKENS * WIDTH * WIDE
    narrow = shape((TOKENS, HEAD), half)
    narrow_full = shape((TOKENS, HEAD), full)
    square = shape((TOKENS, WIDTH), half)

    input_blocks = gather_tp(inputs)
    hot, bias_0, bias_1 = call(
        bias_operands,
        "bias_operands",
        dot_flops // 16,
        (bias_table.reshape(2, BUCKETS), stamps),
        [scalars, whole],
        [narrow] * 3,
        [],
    )
    mix = after(weight_out[0], input_blocks[3], hot)
    mix_near, mix_other = first_way(mix), other_way(mix)
    rows_all, normed_0, proj_0, act_0, gated_0 = call(
        first_forward,
        "first_forward",
        3 * dot_flops,
        (device, lengths, hot, bias_0, *input_blocks, weight_in[0]),
        [scalars] * 2 + [whole] * 11,
        [square, square, shape((TOKENS, WIDE), full), shape((TOKENS, WIDE), half), narrow],
        attention_scratch,
    )
    gated_blocks = gather_tp(gated_0)
    weights_0, slope_0, proj_slope_0, attended_0, inverse_0 = call(
        first_again,
        "first_again",
        2 * dot_flops,
        (lengths, hot, bias_0, proj_0, act_0),
        [scalars] + [whole] * 4,
        [square, square, shape((TOKENS, WIDE), half), narrow_full, narrow_full],
        attention_scratch,
    )
    mix_near = after(mix_near, weights_0)
    mix_blocks = [mix, mix_near, mix_other, first_way(mix_near)]
    mix_blocks += [swap(block) for block in mix_blocks]
    cot = after(cotangent, mix_blocks[3])
    cot_blocks = [cot, first_way(cot), other_way(cot), across(cot)]
    mix_all, product = call(
        products,
        "products",
        dot_flops,
        (*mix_blocks, weight_in[1]),
        [whole] * 9,
        [square, shape((WIDTH, WIDE), half)],
        [],
    )
    wide_full = shape((TOKENS, WIDE), full)
    wide_half = shape((TOKENS, WIDE), half)
    (
        normed_1,
        deviation_1,
        proj_1,
        proj_slope_1,
        act_1,
        weights_1,
        slope_1,
        attended_1,
        inverse_1,
        gated_1,
    ) = call(
        second_forward,
        "second_forward",
        6 * dot_flops,
        (lengths, hot, bias_1, rows_all, *gated_blocks, mix_all, weight_in[1]),
        [scalars] + [whole] * 13,
        [
            square,
            narrow_full,
            wide_full,
            wide_half,
            wide_half,
            square,
            square,
            narrow_full,
            narrow_full,
            narrow,
        ],
        [pltpu.VMEM((TOKENS, WIDTH), half), *attention_scratch],
    )
    cot_blocks += [swap(after(block, gated_1)) for block in cot_blocks]
    message = shape((4 * MESSAGE, HEAD), half)
    cot_all, grad_1, scaled_1, send, keep = call(
        second_backward,
        "second_backward",
        6 * dot_flops,
        (
            device,
            lengths,
            *cot_blocks,
            weight_in[1],
            weight_out[1],
            product,
            deviation_1,
            proj_1,
            proj_slope_1,
            act_1,
            weights_1,
            slope_1,
            attended_1,
            inverse_1,
        ),
        [scalars] * 2 + [whole] * 19,
        [square, wide_half, wide_half, message, message],
        [
            pltpu.VMEM((TOKENS, HEAD), full),
            pltpu.VMEM((TOKENS, HEAD), full),
            pltpu.VMEM((16, HEAD), full),
        ],
    )
    gated_parts, gated_sums = scatter_tp(send, keep, "gated_pairs")
    out_send, out_keep = (
        call(
            out_partials,
            f"out_partials_{name}",
            dot_flops,
            (*blocks, scaled, weight_in[1]),
            [whole] * 6,
            [shape((4 * HEAD, WIDTH), half)],
            [],
        )[0]
        for name, blocks, scaled in (
            ("send", gated_blocks[4:], scaled_1),
            ("keep", gated_blocks[:4], after(scaled_1, gated_sums)),
        )
    )
    out_parts, _ = scatter_tp(out_send, out_keep, "out_pairs")
    merged_shapes = [shape((WIDTH, WIDE), full), shape((HEAD, WIDTH), full)]
    merged_in_1, merged_out_1, left_1 = call(
        second_merge,
        "second_merge",
        3 * dot_flops,
        (
            after(normed_1, gated_sums),
            grad_1,
            gated_1,
            cot_all,
            error_in,
            error_out,
            factor_in,
            factor_out,
        ),
        [whole] * 4
        + [
            layer_block((WIDTH, WIDE), 1),
            layer_block((HEAD, WIDTH), 1),
            layer_block((RANK, WIDE), 1),
            layer_block((RANK, WIDTH), 1),
        ],
        merged_shapes + [shape((RANK, WIDTH + HEAD), half)],
        [],
        [whole] * 3,
    )
    below_0, upstream_0, out_0, row_sums = call(
        first_sides,
        "first_sides",
        dot_flops,
        (normed_1, after(cot_all, gated_sums), gated_0, weight_out[0]),
        [whole] * 4,
        [narrow_full, narrow_full, shape((HEAD, WIDTH), full), shape((16, HEAD), full)],
        [],
    )

    left_1 = sum_z(left_1, "left_sum_1")
    merged_in_0, left_in_0 = call(
        first_backward,
        "first_backward",
        6 * dot_flops,
        (
            lengths,
            *gated_parts,
            weights_0,
            slope_0,
            proj_slope_0,
            attended_0,
            inverse_0,
            upstream_0,
            row_sums,
            after(below_0, left_1),
            act_0,
            normed_0,
            error_in,
            factor_in,
        ),
        [scalars] + [whole] * 14 + [layer_block((WIDTH, WIDE), 0), layer_block((RANK, WIDE), 0)],
        [shape((WIDTH, WIDE), full), shape((RANK, WIDTH), half)],
        [
            pltpu.VMEM((TOKENS, WIDE), half),
            pltpu.VMEM((TOKENS, HEAD), full),
            pltpu.VMEM((TOKENS, HEAD), full),
        ],
        [whole] * 2,
    )
    left_parts_1 = ring_x(left_1)
    merged_out_0, left_0 = call(
        first_merge,
        "first_merge",
        dot_flops // 4,
        (gated_0, out_0, normed_1, *gated_parts, *out_parts, error_out, factor_out, after(left_in_0, left_parts_1[1])),
        [whole] * 11 + [layer_block((HEAD, WIDTH), 0), layer_block((RANK, WIDTH), 0), whole],
        [shape((HEAD, WIDTH), full), shape((RANK, WIDTH + HEAD), half)],
        [pltpu.VMEM((TOKENS, HEAD), half)],
        [whole] * 2,
    )
    left_0 = sum_z(left_0, "left_sum_0")
    outs = compress(left_parts_1, (merged_in_1, merged_out_1), 1, ())
    outs = compress(ring_x(left_0), (merged_in_0, merged_out_0), 0, tuple(outs))
    update_in, update_out, next_in, next_out, error_in_next, error_out_next = outs
    return (
        update_in.reshape(2, 1, WIDTH, WIDE),
        update_out.reshape(2, 1, HEAD, WIDTH),
        next_in.reshape(2, 1, RANK, WIDE),
        next_out.reshape(2, 1, RANK, WIDTH),
        error_in_next.reshape(1, 2, 1, WIDTH, WIDE),
        error_out_next.reshape(1, 2, 1, HEAD, WIDTH),
    )


def solution(mesh):
    placed_in = (
        P(("rep", "tp"), None),
        P(("rep", "tp"), None),
        P(None, None, None, "tp", None),
        P(None, "tp", None, None),
        P(None, "tp", None),
        P("rep"),
        P("rep", None),
        P(None, "tp", None, None),
        P(None, "tp", None, None),
        P("rep", None, "tp", None, None),
        P("rep", None, "tp", None, None),
    )
    return jax.shard_map(
        per_device,
        mesh=mesh,
        in_specs=placed_in,
        out_specs=(
            P(None, "tp", None, None),
            P(None, "tp", None, None),
            P(None, "tp", None, None),
            P(None, "tp", None, None),
            P("rep", None, "tp", None, None),
            P("rep", None, "tp", None, None),
        ),
        check_vma=False,
    )
```
